512 devices in a mesh: seq: 128 (over z, x, core), tp: 4 (over y).
Axes of the slice: x: 4, y: 4, z: 16, core: 2. Of those that a mesh axis runs over, the one named last changes fastest.
Arguments:
- byte_states: bfloat16 [131072, 1024], P(('seq', 'tp')), may hold values from -24 to 24
- cotangent: bfloat16 [131072, 1024], P(('seq', 'tp')), may hold values from -0.125 to 0.125
- w_up: bfloat16 [1024, 2048], P('seq', 'tp'), may hold values from -0.1875 to 0.1875
- w_down: bfloat16 [2048, 1024], P('tp', 'seq'), may hold values from -0.125 to 0.125
- bounds: int32 [131072], P('seq'), may hold values from 0 to 1, as said below
- owner_counts: int32 [128], replicated, may hold values from 128 to 448, as said below
Outputs:
- hidden: bfloat16 [65536, 2048], P('seq', 'tp')
- grad_up: float32 [1024, 2048], P('seq', 'tp')
- grad_down: float32 [2048, 1024], P('tp', 'seq')
The draws below stay inside these ranges and needn't reach their ends.
Inputs may be any that keep to these rules, and one draw needn't show every extreme that they name: `bounds`: the first byte of every device's 256 bytes starts a span. The bytes of one device hold at most 96 span starts, and some device holds exactly 96. `owner_counts`: the counts sum to the number of ones in bounds. Owner o's spans are those that start in the bytes of group o (bytes o * 1024 to (o + 1) * 1024 - 1), with at most 32 spans taken from or given to the group before and likewise at the group after; owner 0 begins with span 0; somewhere exactly 32 spans change hands between two neighbouring groups; some owner holds exactly 448 spans.
All inputs are finite; a program needn't handle non-finite values.
Results may differ from the reference program's by a relative error of at most 0.006.
Values may be sent and summed in bfloat16 or wider, within the bound.
A program may use at most 64 MiB of HBM per device.

```python
import jax
import jax.numpy as jnp
from jax import lax

DB = 1024
DC = 2048
BD = 256
KLOC = 96
MOVE = 32
GROUPS = 128
SLICES = 4
GB = 1024
BYTES = 131072
CAP = 512


def span_plan(key):
    subkeys = jax.random.split(key, 6)
    devices_all = GROUPS * SLICES
    forced = jax.random.randint(subkeys[5], (), 1, GROUPS - 1)
    lower_draws = jax.random.randint(subkeys[0], (devices_all,), KLOC // 2, KLOC)
    dense_rows = jax.random.randint(subkeys[1], (devices_all,), 0, 8) == 0
    device_group = jnp.arange(devices_all) // SLICES
    counts = jnp.where(dense_rows | (device_group == forced), KLOC, lower_draws)
    orders = jax.vmap(lambda one_key: jax.random.permutation(one_key, BD))(jax.random.split(subkeys[3], devices_all))
    scores = (orders - orders[:, :1]) % BD
    marks = (scores < counts[:, None]).astype(jnp.int32)
    group_sizes = counts.reshape(GROUPS, SLICES).sum(axis=1)
    interior = jax.random.randint(subkeys[4], (GROUPS - 1,), -MOVE, MOVE + 1)
    positions = jnp.arange(GROUPS - 1)
    interior = jnp.where(positions == forced, MOVE, interior)
    interior = jnp.where(positions == forced - 1, -MOVE, interior)
    edge_zero = jnp.zeros((1,), jnp.int32)
    shifts = jnp.concatenate([edge_zero, interior.astype(jnp.int32), edge_zero])
    owners = group_sizes + shifts[1:] - shifts[:-1]
    return (marks.reshape(BYTES).astype(jnp.int32), owners.astype(jnp.int32))


def draw_bounds(key, part):
    planned = span_plan(key)
    return planned[0]


def draw_owner_counts(key, part):
    planned = span_plan(key)
    return planned[1]


def raised(drawn, stream_key, source, target, parts, factor):
    owner, partner = [(jnp.arange(drawn.shape[dim]) // (drawn.shape[dim] // parts)).reshape([-1 if axis == dim else 1 for axis in range(drawn.ndim)]) for dim in (source, target)]
    chosen = jax.random.permutation(stream_key, parts)[partner]
    strong = (owner == chosen) | (owner == (partner + parts // 2) % parts)
    return jnp.where(strong, factor * drawn, drawn)


def level_of(key, dims, pieces, low, top_value):
    def one(axis_at, shards_of):
        heights = jax.random.uniform(jax.random.fold_in(jax.random.fold_in(key, 6), axis_at), (shards_of,), jnp.float32, low / len(pieces), top_value / len(pieces))
        return jnp.repeat(jnp.exp(heights), dims[axis_at] // shards_of).reshape((-1,) + (1,) * (len(dims) - axis_at - 1))

    loudness = one(*pieces[0])
    for cut in pieces[1:]:
        loudness = loudness * one(*cut)
    return loudness


def scatter_about(stream_key, dims, deviation, bound, cuts=(), kind=jnp.bfloat16):
    entries = deviation * jax.random.normal(stream_key, dims, jnp.float32)
    if cuts:
        entries = entries * level_of(stream_key, dims, cuts, -0.22, 0.18)
    return jnp.clip(entries, -bound, bound).astype(kind)


def bell_draw_with(stream_key, extent, deviation, most, cuts, heavy, held_as=jnp.bfloat16):
    result = deviation * jax.random.normal(stream_key, extent, jnp.float32)
    if cuts:
        result = result * level_of(stream_key, extent, cuts, -0.22, 0.18)
    return jnp.clip(raised(result, jax.random.fold_in(stream_key, 3), *heavy), -most, most).astype(held_as)


def setup_inputs(seed: int = 0) -> dict:
    streams_of = jax.random.split(jax.random.key(seed), 7)
    return {
        "byte_states": bell_draw_with(streams_of[0], (BYTES, DB), 1.0, 24.0, ((0, 512),), (0, 1, 512, 6.0)),
        "cotangent": bell_draw_with(streams_of[1], (BYTES, DB), (2.0 / BYTES ** 0.5), 0.125, ((0, 512),), (0, 1, 512, 6.0)),
        "w_up": scatter_about(streams_of[2], (DB, DC), DB ** -0.5, 0.1875, ((0, 128), (1, 4))),
        "w_down": scatter_about(streams_of[3], (DC, DB), DC ** -0.5, 0.125, ((0, 4), (1, 128))),
        "bounds": draw_bounds(jax.random.fold_in(streams_of[6], 71), 0),
        "owner_counts": draw_owner_counts(jax.random.fold_in(streams_of[6], 71), 0),
    }


epsilon = 1e-05

def reference(byte_states, cotangent, w_up, w_down, bounds, owner_counts):
    span_of = (jnp.cumsum(bounds) - 1).astype(jnp.int32)
    starts = jnp.nonzero(bounds, size=BYTES, fill_value=0)[0].astype(jnp.int32)
    owner_first = (jnp.cumsum(owner_counts) - owner_counts).astype(jnp.int32)
    row_ids = jnp.arange(CAP, dtype=jnp.int32)

    def one_owner(totals, owner_index):
        grad_up, grad_down = totals
        first_span = owner_first[owner_index]
        owned_count = owner_counts[owner_index]
        live_rows = row_ids < owned_count
        span_ids = jnp.where(live_rows, first_span + row_ids, 0).astype(jnp.int32)
        picked = jnp.take(byte_states, starts[span_ids], axis=0).astype(jnp.float32)
        inverse_rms = lax.rsqrt(lax.optimization_barrier(jnp.mean(picked * picked, axis=1, keepdims=True)) + epsilon)
        normed = jnp.where(live_rows[:, None], picked * inverse_rms, jnp.float32(0.0)).astype(jnp.bfloat16)
        preact = jnp.dot(normed, w_up, preferred_element_type=jnp.float32)
        hidden = jax.nn.silu(preact).astype(jnp.bfloat16)
        window_start = jnp.clip((owner_index - 1) * GB, 0, BYTES - 3 * GB).astype(jnp.int32)
        cot_window = lax.dynamic_slice_in_dim(cotangent, window_start, 3 * GB, 0).astype(jnp.float32)
        segment_ids = lax.dynamic_slice_in_dim(span_of, window_start, 3 * GB, 0) - first_span
        segment_ids = jnp.where((segment_ids >= 0) & (segment_ids < owned_count), segment_ids, CAP).astype(jnp.int32)
        cot_sums = jax.ops.segment_sum(cot_window, segment_ids, num_segments=CAP + 1)[:CAP]
        span_cot = cot_sums.astype(jnp.bfloat16)
        grad_down = grad_down + jnp.dot(hidden.T, span_cot, preferred_element_type=jnp.float32)
        back_grad = jnp.dot(span_cot, w_down.T, preferred_element_type=jnp.float32)
        gate_sigmoid = jax.nn.sigmoid(preact)
        preact_grad = (back_grad * gate_sigmoid * (1.0 + preact * (1.0 - gate_sigmoid))).astype(jnp.bfloat16)
        grad_up = grad_up + jnp.dot(normed.T, preact_grad, preferred_element_type=jnp.float32)
        return ((grad_up, grad_down), hidden)
    initial = (jnp.zeros((DB, DC), jnp.float32), jnp.zeros((DC, DB), jnp.float32))
    (grad_up, grad_down), hidden = lax.scan(one_owner, initial, jnp.arange(GROUPS, dtype=jnp.int32))
    return (hidden.reshape(GROUPS * CAP, DC), grad_up, grad_down)
```

```python
import functools

import jax
import jax.numpy as jnp
from jax import lax
from jax.experimental import pallas as pl
from jax.experimental.pallas import tpu as pltpu
from jax.sharding import PartitionSpec as P

MESH = pl.DeviceIdType.MESH
F32 = jnp.float32
BF16 = jnp.bfloat16

KLOC = 96
SLOT = 128
HALF = KLOC // 2
MOVE = 32
NX, NY, NZ = 4, 4, 16
BD = 256
DB = 1024
CW = 256
CAP = 512
NONE = -1.0e6
epsilon = 1e-05


def dot(a, b):
    return jnp.dot(a, b, preferred_element_type=F32)


def dot_nt(a, b):
    return lax.dot_general(a, b, (((1,), (1,)), ((), ())), preferred_element_type=F32)


def iota(shape, dim):
    return lax.broadcasted_iota(jnp.int32, shape, dim)


def kernel(
    bs_hbm, co_hbm, wu_in, wd_in, marks_in, oc_in,
    hid_hbm, gu_out, gd_out,
    bs, co, pw, rw, wu, wd, xn, xc, nt, ct, hh, pg, ff,
    gu32, gub, gd32, gdb,
    ux, ua, ub, u1, u1b, u2, u2b,
    dx, da, db, d1, d1b, d2, d2b,
    hs, hr, ho, hq, fs, fr,
    in_sem, out_sem,
    w_ss, w_rs, ub_ss, ub_rs, ua_ss, ua_rs, ux_ss, ux_rs,
    db_ss, db_rs, da_ss, da_rs, dx_ss, dx_rs,
    y_ss, y_rs, s_ss, s_rs,
    gux_ss, gux_rs, gua_ss, gua_rs, gub_ss, gub_rs,
    gdx_ss, gdx_rs, gda_ss, gda_rs, gdb_ss, gdb_rs,
    h_ss, h_rs, f_ss, f_rs,
):
    s = lax.axis_index("seq")
    t = lax.axis_index("tp")
    c = s % 2
    k = s // 2
    x = k % NX
    z = k // NX
    zm = z % 4
    zh = z // 4
    oc = 1 - c

    def at(zz, xx, cc, tt):
        return (((zz + NZ) % NZ * NX + (xx + NX) % NX) * 2 + cc, (tt + NY) % NY)

    sib = at(z, x, oc, t)
    yp, ym = at(z, x, c, t + 1), at(z, x, c, t - 1)
    xs = [at(z, x + 1, c, t), at(z, x - 1, c, t), at(z, x + 2, c, t)]
    za = [at(z + 1, x, c, t), at(z - 1, x, c, t), at(z + 2, x, c, t), at(z - 2, x, c, t)]
    zb = [at(z + 4, x, c, t), at(z - 4, x, c, t), at(z + 8, x, c, t)]
    nk = NZ * NX
    k_next = ((k + 1) % nk * 2 + c, t)
    k_prev = ((k + nk - 1) % nk * 2 + c, t)

    sends = []

    def send(src, dst, ss, rs, to):
        cp = pltpu.make_async_remote_copy(
            src_ref=src, dst_ref=dst, send_sem=ss, recv_sem=rs, device_id=to, device_id_type=MESH
        )
        cp.start()
        sends.append(cp)
        return cp

    in_bs = pltpu.make_async_copy(bs_hbm, bs, in_sem.at[0])
    in_co = pltpu.make_async_copy(co_hbm, co, in_sem.at[1])
    in_bs.start()
    in_co.start()
    peers = [sib, yp, ym] + xs + za + zb + [k_next, k_prev]
    barrier = pltpu.get_barrier_semaphore()
    for p in peers:
        pl.semaphore_signal(barrier, inc=1, device_id=p, device_id_type=MESH)

    marks = marks_in[...].astype(F32)
    row8 = iota((8, 128), 0)
    lane8 = iota((8, 128), 1)
    own_marks = jnp.concatenate(
        [
            jnp.sum(jnp.where(row8 == 2 * t + h, marks, 0.0), axis=0, keepdims=True)
            for h in range(2)
        ],
        axis=1,
    )
    upto = (iota((BD, BD), 0) <= iota((BD, BD), 1)).astype(F32).astype(BF16)
    rank = dot(jnp.broadcast_to(own_marks, (16, BD)).astype(BF16), upto)[0:1]
    slot_ids = iota((KLOC, BD), 0).astype(F32)
    in_span = jnp.where(slot_ids == rank - 1.0, 1.0, 0.0)
    segment = in_span.astype(BF16)
    select = (in_span * own_marks).astype(BF16)

    per_row = jnp.sum(marks, axis=1, keepdims=True)
    own_counts = jnp.sum(
        jnp.where(row8 // 2 + 4 * c == lane8, per_row, 0.0), axis=0, keepdims=True
    )
    counts16 = jnp.broadcast_to(own_counts, (16, 128)).astype(BF16)
    both_w = jnp.concatenate([wu_in[...].astype(F32), wd_in[...].astype(F32)], axis=0).astype(BF16)
    for h in range(2):
        pw[h, :, 0:CW] = both_w[:, h * CW : (h + 1) * CW]
        pw[h, :, CW : CW + 128] = counts16

    in_bs.wait()
    picked = dot(select, bs[...])
    inverse_rms = lax.rsqrt(jnp.mean(picked * picked, axis=1, keepdims=True) + epsilon)
    xn[c, t] = (picked * inverse_rms).astype(BF16)

    pl.semaphore_wait(barrier, len(peers))

    w_cp = send(pw.at[oc], rw, w_ss, w_rs, sib)

    def send_own(buf, kind):
        own = buf.at[c, t]
        return (
            send(own, own, y_ss.at[kind, 0], y_rs.at[kind, 0], yp),
            send(own, own, y_ss.at[kind, 1], y_rs.at[kind, 1], ym),
            send(own, own, s_ss.at[kind, 0], s_rs.at[kind, 0], sib),
        )

    own_n = send_own(xn, 0)
    in_co.wait()
    xc[c, t] = dot(segment, co[...]).astype(BF16)
    own_c = send_own(xc, 1)

    tp_, tm_, t2_ = (t + 1) % NY, (t + NY - 1) % NY, (t + 2) % NY

    def forward(buf, kind, own):
        own[0].wait_recv()
        a = buf.at[c, tm_, 0:HALF]
        f0 = send(a, a, y_ss.at[kind, 2], y_rs.at[kind, 2], yp)
        a = buf.at[c, tm_]
        g0 = send(a, a, s_ss.at[kind, 1], s_rs.at[kind, 1], sib)
        own[1].wait_recv()
        a = buf.at[c, tp_, HALF:KLOC]
        f1 = send(a, a, y_ss.at[kind, 3], y_rs.at[kind, 3], ym)
        a = buf.at[c, tp_]
        g1 = send(a, a, s_ss.at[kind, 2], s_rs.at[kind, 2], sib)
        return f0, f1, g0, g1

    def forward_far(buf, kind, f):
        f[0].wait_recv()
        a = buf.at[c, t2_, 0:HALF]
        g2 = send(a, a, s_ss.at[kind, 3], s_rs.at[kind, 3], sib)
        f[1].wait_recv()
        a = buf.at[c, t2_, HALF:KLOC]
        g3 = send(a, a, s_ss.at[kind, 4], s_rs.at[kind, 4], sib)
        return g2, g3

    eye = (iota((256, 256), 0) == iota((256, 256), 1)).astype(F32).astype(BF16)
    filler = jnp.zeros((SLOT - KLOC, DB), BF16)

    def rows_of(buf, cc, tt):
        return jnp.concatenate([buf[cc, tt], filler], axis=0)

    def transpose(buf, out, cc, tt):
        rows = rows_of(buf, cc, tt)
        for j in range(DB // 256):
            out[cc * 4 + tt, j * 256 : (j + 1) * 256, :] = dot_nt(
                eye, rows[:, j * 256 : (j + 1) * 256]
            ).astype(BF16)

    def up(cc, tt):
        v = dot(rows_of(xn, cc, tt), wu[...].reshape(DB, CW))
        sg = jax.nn.sigmoid(v)
        hh[cc * 4 + tt] = (v * sg).astype(BF16)
        ff[cc * 4 + tt] = sg * (1.0 + v * (1.0 - sg))

    def back(cc, tt):
        v = dot(rows_of(xc, cc, tt), wd[:, :, :, :, 0:CW].reshape(DB, CW))
        pg[cc * 4 + tt] = (v * ff[cc * 4 + tt]).astype(BF16)

    w_cp.wait_recv()
    mine, other = pw[c].astype(F32), rw[...].astype(F32)
    low, high = jnp.where(c == 0, mine, other), jnp.where(c == 0, other, mine)
    wu[zh, zm, x] = jnp.concatenate([low[0:8, 0:CW], high[0:8, 0:CW]], axis=0).astype(BF16)
    counts_f = low[0:8, CW:] + high[0:8, CW:]
    wd[zh, zm, x, :, 0:CW] = jnp.concatenate([low[8:16, 0:CW], high[8:16, 0:CW]], axis=0).astype(BF16)
    wd[zh, zm, x, :, CW:] = jnp.concatenate([counts_f, counts_f], axis=0).astype(BF16)

    def gather_zb(buf, ss, rs):
        a = buf.at[zh, zm, x]
        return [send(a, a, ss.at[j], rs.at[j], zb[j]) for j in range(3)]

    def gather_za(parts, ss, rs):
        full, first, second = parts
        return [
            send(full, full, ss.at[0], rs.at[0], za[0]),
            send(full, full, ss.at[1], rs.at[1], za[1]),
            send(first, first, ss.at[2], rs.at[2], za[2]),
            send(second, second, ss.at[3], rs.at[3], za[3]),
        ]

    def gather_x(a, ss, rs):
        return [send(a, a, ss.at[j], rs.at[j], xs[j]) for j in range(3)]

    def arrive(cps):
        for cp in cps:
            cp.wait_recv()

    w_u = gather_zb(wu, ub_ss, ub_rs)
    w_d = gather_zb(wd, db_ss, db_rs)
    transpose(xn, nt, c, t)
    transpose(xc, ct, c, t)
    arrive(w_u)
    w_u = gather_za(
        (wu.at[:, zm, x], wu.at[0:2, zm, x], wu.at[2:4, zm, x]), ua_ss, ua_rs
    )
    arrive(w_d)
    w_d = gather_x(wd.at[:, zm, x], dx_ss, dx_rs)

    far_n = forward(xn, 0, own_n)
    arrive(w_u)
    w_u = gather_x(wu.at[:, :, x], ux_ss, ux_rs)
    arrive(w_d)
    w_d = gather_za((wd.at[:, zm], wd.at[0:2, zm], wd.at[2:4, zm]), da_ss, da_rs)
    own_n[2].wait_recv()
    transpose(xn, nt, oc, t)
    transpose(xn, nt, c, tm_)
    transpose(xn, nt, c, tp_)

    far_c = forward(xc, 1, own_c)
    own_c[2].wait_recv()
    transpose(xc, ct, oc, t)
    transpose(xc, ct, c, tm_)
    transpose(xc, ct, c, tp_)
    far_n[2].wait_recv()
    far_n[3].wait_recv()
    transpose(xn, nt, oc, tm_)
    transpose(xn, nt, oc, tp_)

    arrive(w_u)
    last_n = forward_far(xn, 0, far_n)
    for cc, tt in ((c, t), (oc, t), (c, tm_), (c, tp_), (oc, tm_), (oc, tp_), (c, t2_)):
        up(cc, tt)
    transpose(xn, nt, c, t2_)
    arrive(w_d)
    last_c = forward_far(xc, 1, far_c)
    far_c[2].wait_recv()
    far_c[3].wait_recv()
    transpose(xc, ct, oc, tm_)
    transpose(xc, ct, oc, tp_)
    transpose(xc, ct, c, t2_)
    for cc, tt in ((c, t), (oc, t), (c, tm_), (c, tp_), (oc, tm_), (oc, tp_), (c, t2_)):
        back(cc, tt)
    last_n[0].wait_recv()
    last_n[1].wait_recv()
    up(oc, t2_)
    transpose(xn, nt, oc, t2_)
    last_c[0].wait_recv()
    last_c[1].wait_recv()
    transpose(xc, ct, oc, t2_)

    def grad(tt_ref, right_ref, g32, gb):
        right = right_ref[...].reshape(8 * SLOT, CW)
        for i in range(4):
            left = jnp.concatenate(
                [tt_ref[b, i * 256 : (i + 1) * 256, :] for b in range(8)], axis=1
            )
            r = dot(left, right).reshape(4, NX, 16, CW)
            g32[i] = r
            gb[i] = r.astype(BF16)

    c1, c2, c3 = (zm + 1) % 4, (zm + 2) % 4, (zm + 3) % 4
    x1, x2, x3 = (x + 1) % 4, (x + 2) % 4, (x + 3) % 4
    h1, h2, h3 = (zh + 1) % 4, (zh + 2) % 4, (zh + 3) % 4

    def scatter_za(buf, rest, into, ss, rs):
        def part(zs, m):
            return buf.at[zs, m] if rest is None else buf.at[zs, m, rest]

        allz, lo, hi = slice(0, 4), slice(0, 2), slice(2, 4)
        return [
            send(part(allz, c1), into.at[0], ss.at[0], rs.at[0], za[0]),
            send(part(allz, c3), into.at[1], ss.at[1], rs.at[1], za[1]),
            send(part(lo, c2), into.at[2, 0:2], ss.at[2], rs.at[2], za[2]),
            send(part(hi, c2), into.at[2, 2:4], ss.at[3], rs.at[3], za[3]),
        ]

    def scatter_zb(buf, into, ss, rs):
        return [
            send(buf.at[h1], into.at[0], ss.at[0], rs.at[0], zb[0]),
            send(buf.at[h3], into.at[1], ss.at[1], rs.at[1], zb[1]),
            send(buf.at[h2], into.at[2], ss.at[2], rs.at[2], zb[2]),
        ]

    def total(own, into):
        return own + into[0].astype(F32) + into[1].astype(F32) + into[2].astype(F32)

    grad(ct, hh, gd32, gdb)
    g_d = scatter_za(gdb, None, da, gda_ss, gda_rs)
    back(oc, t2_)
    grad(nt, pg, gu32, gub)
    g_u = [
        send(gub.at[:, :, xx], ux.at[j], gux_ss.at[j], gux_rs.at[j], xs[j])
        for j, xx in enumerate((x1, x3, x2))
    ]

    chips = wd[:, :, :, :, CW:].reshape(NZ * NX * 16, 128).astype(F32)
    chip_row = iota((NZ * NX * 16, 128), 0)
    chip_lane = iota((NZ * NX * 16, 128), 1)
    first_rows = chip_row % 16 == 0
    ahead = jnp.where(first_rows & (chip_row // 16 < k) & (chip_lane < 8), chips, 0.0)
    before_a = jnp.sum(jnp.sum(ahead, axis=0, keepdims=True), axis=1, keepdims=True)
    here = jnp.sum(
        jnp.where(first_rows & (chip_row // 16 == k), chips, 0.0), axis=0, keepdims=True
    )
    lane1 = iota((1, 128), 1)
    slot1 = lane1.astype(F32)
    pos, totals = [], []
    for g in range(2):
        first = jnp.zeros((1, 1), F32)
        parts = []
        for p in range(4):
            n = jnp.sum(jnp.where(lane1 == 4 * g + p, here, 0.0), axis=1, keepdims=True)
            parts.append(jnp.where(slot1 < n, slot1 + first, NONE))
            first = first + n
        pos.append(jnp.concatenate(parts, axis=1))
        totals.append(first)
    owners = oc_in[...].astype(F32)
    owner_first = jnp.sum(jnp.where(lane1 < 2 * k, owners, 0.0), axis=1, keepdims=True)
    owned = [
        jnp.sum(jnp.where(lane1 == 2 * k + g, owners, 0.0), axis=1, keepdims=True)
        for g in range(2)
    ]
    shift = [owner_first - before_a, owner_first + owned[0] - before_a - totals[0]]
    end_ids = iota((MOVE, CAP), 0).astype(F32)
    group_rows = [hh[4 * g : 4 * g + 4].reshape(CAP, CW) for g in range(2)]

    def ends(g, base):
        table = jnp.where(end_ids + base == pos[g], 1.0, 0.0).astype(BF16)
        return dot(table, group_rows[g]).astype(BF16)

    hs[0] = ends(0, 0.0)
    hs[1] = ends(1, totals[1] - MOVE)
    h_p = send(hs.at[0], hr.at[0], h_ss.at[0], h_rs.at[0], k_prev)
    h_n = send(hs.at[1], hr.at[1], h_ss.at[1], h_rs.at[1], k_next)
    first_b = ends(1, 0.0)
    last_a = ends(0, totals[0] - MOVE)

    row_ids = iota((CAP, CAP), 0).astype(F32)
    end_row = iota((CAP, 2 * MOVE), 0).astype(F32)
    end_lane1 = iota((1, 2 * MOVE), 1)
    end_at = end_lane1.astype(F32)

    def place(g, edge):
        inner = jnp.where(
            (row_ids + shift[g] == pos[g]) & (row_ids < owned[g]), 1.0, 0.0
        ).astype(BF16)
        end_pos = jnp.where(end_lane1 < MOVE, end_at - MOVE, end_at - MOVE + totals[g])
        outer = jnp.where(
            (end_row + shift[g] == end_pos) & (end_row < owned[g]), 1.0, 0.0
        ).astype(BF16)
        ho[g] = (dot(inner, group_rows[g]) + dot(outer, edge)).astype(BF16)

    h_p.wait_recv()
    h_n.wait_recv()
    place(0, jnp.concatenate([hr[1], first_b], axis=0))
    place(1, jnp.concatenate([last_a, hr[0]], axis=0))
    h_s = send(ho.at[oc], hq, h_ss.at[2], h_rs.at[2], sib)
    out_own = pltpu.make_async_copy(
        ho.at[c], hid_hbm.at[:, pl.ds(pl.multiple_of(c * CW, CW), CW)], out_sem.at[0]
    )
    out_own.start()

    arrive(g_d)
    r = total(gd32[:, zm], da)
    d1[...] = r
    d1b[...] = r.astype(BF16)
    g_d = [
        send(d1b.at[:, xx], dx.at[j], gdx_ss.at[j], gdx_rs.at[j], xs[j])
        for j, xx in enumerate((x1, x3, x2))
    ]
    arrive(g_u)
    r = total(gu32[:, :, x], ux)
    u1[...] = r
    u1b[...] = r.astype(BF16)
    g_u = scatter_za(u1b, None, ua, gua_ss, gua_rs)

    arrive(g_d)
    r = total(d1[:, x], dx)
    d2[...] = r
    d2b[...] = r.astype(BF16)
    g_d = scatter_zb(d2b, db, gdb_ss, gdb_rs)
    arrive(g_u)
    r = total(u1[:, zm], ua)
    u2[...] = r
    u2b[...] = r.astype(BF16)
    g_u = scatter_zb(u2b, ub, gub_ss, gub_rs)

    h_s.wait_recv()
    out_sib = pltpu.make_async_copy(
        hq, hid_hbm.at[:, pl.ds(pl.multiple_of(oc * CW, CW), CW)], out_sem.at[1]
    )
    out_sib.start()

    arrive(g_d)
    r = total(d2[zh], db)
    fs[1, 0] = r[0:8]
    fs[1, 1] = r[8:16]
    arrive(g_u)
    r = total(u2[zh], ub)
    fs[0, 0] = r[0:8]
    fs[0, 1] = r[8:16]
    f_cp = send(fs.at[:, oc], fr, f_ss, f_rs, sib)
    f_cp.wait_recv()
    for i, out in enumerate((gu_out, gd_out)):
        mine, other = fs[i, c], fr[i]
        out[:, 0:CW] = jnp.where(c == 0, mine, other)
        out[:, CW:] = jnp.where(c == 0, other, mine)

    for cp in sends:
        cp.wait_send()
    out_own.wait()
    out_sib.wait()


def body(byte_states, cotangent, w_up, w_down, bounds, owner_counts):
    vmem = pl.BlockSpec(memory_space=pltpu.VMEM)
    hbm = pl.BlockSpec(memory_space=pl.ANY)
    dma = pltpu.SemaphoreType.DMA
    scratch = [
        pltpu.VMEM((BD, DB), BF16),
        pltpu.VMEM((BD, DB), BF16),
        pltpu.VMEM((2, 16, CW + 128), BF16),
        pltpu.VMEM((16, CW + 128), BF16),
        pltpu.VMEM((4, 4, NX, 16, CW), BF16),
        pltpu.VMEM((4, 4, NX, 16, CW + 128), BF16),
        pltpu.VMEM((2, NY, KLOC, DB), BF16),
        pltpu.VMEM((2, NY, KLOC, DB), BF16),
        pltpu.VMEM((8, DB, SLOT), BF16),
        pltpu.VMEM((8, DB, SLOT), BF16),
        pltpu.VMEM((8, SLOT, CW), BF16),
        pltpu.VMEM((8, SLOT, CW), BF16),
        pltpu.VMEM((8, SLOT, CW), F32),
        pltpu.VMEM((4, 4, NX, 16, CW), F32),
        pltpu.VMEM((4, 4, NX, 16, CW), BF16),
        pltpu.VMEM((4, 4, NX, 16, CW), F32),
        pltpu.VMEM((4, 4, NX, 16, CW), BF16),
        pltpu.VMEM((3, 4, 4, 16, CW), BF16),
        pltpu.VMEM((3, 4, 16, CW), BF16),
        pltpu.VMEM((3, 16, CW), BF16),
        pltpu.VMEM((4, 4, 16, CW), F32),
        pltpu.VMEM((4, 4, 16, CW), BF16),
        pltpu.VMEM((4, 16, CW), F32),
        pltpu.VMEM((4, 16, CW), BF16),
        pltpu.VMEM((3, 4, 16, CW), BF16),
        pltpu.VMEM((3, 4, NX, 16, CW), BF16),
        pltpu.VMEM((3, 16, CW), BF16),
        pltpu.VMEM((4, NX, 16, CW), F32),
        pltpu.VMEM((4, NX, 16, CW), BF16),
        pltpu.VMEM((4, 16, CW), F32),
        pltpu.VMEM((4, 16, CW), BF16),
        pltpu.VMEM((2, MOVE, CW), BF16),
        pltpu.VMEM((2, MOVE, CW), BF16),
        pltpu.VMEM((2, CAP, CW), BF16),
        pltpu.VMEM((CAP, CW), BF16),
        pltpu.VMEM((2, 2, 8, CW), F32),
        pltpu.VMEM((2, 8, CW), F32),
        dma((2,)),
        dma((2,)),
        dma, dma,
        dma((3,)), dma((3,)), dma((4,)), dma((4,)), dma((3,)), dma((3,)),
        dma((3,)), dma((3,)), dma((4,)), dma((4,)), dma((3,)), dma((3,)),
        dma((2, 4)), dma((2, 4)), dma((2, 5)), dma((2, 5)),
        dma((3,)), dma((3,)), dma((4,)), dma((4,)), dma((3,)), dma((3,)),
        dma((3,)), dma((3,)), dma((4,)), dma((4,)), dma((3,)), dma((3,)),
        dma((3,)), dma((3,)), dma, dma,
    ]
    hidden, grad_up, grad_down = pl.pallas_call(
        kernel,
        out_shape=(
            jax.ShapeDtypeStruct((CAP, 2 * CW), BF16),
            jax.ShapeDtypeStruct((8, 2 * CW), F32),
            jax.ShapeDtypeStruct((8, 2 * CW), F32),
        ),
        in_specs=[hbm, hbm, vmem, vmem, vmem, vmem],
        out_specs=(hbm, vmem, vmem),
        scratch_shapes=scratch,
        compiler_params=pltpu.CompilerParams(
            collective_id=0, has_side_effects=True, vmem_limit_bytes=48 * 1024 * 1024
        ),
        cost_estimate=pl.CostEstimate(
            flops=4 * 10**9, bytes_accessed=2 * 1024 * 1024, transcendentals=262144
        ),
    )(
        byte_states,
        cotangent,
        w_up,
        w_down.T,
        bounds.reshape(8, 128),
        owner_counts.reshape(1, 128),
    )
    return hidden, grad_up, grad_down.T


def solution(mesh):
    return jax.shard_map(
        body,
        mesh=mesh,
        in_specs=(
            P(("seq", "tp"), None),
            P(("seq", "tp"), None),
            P("seq", "tp"),
            P("tp", "seq"),
            P("seq"),
            P(),
        ),
        out_specs=(P("seq", "tp"), P("seq", "tp"), P("tp", "seq")),
        check_vma=False,
    )
```

```python
import functools

import jax
import jax.numpy as jnp
from jax import lax
from jax.experimental import pallas as pl
from jax.experimental.pallas import tpu as pltpu
from jax.sharding import PartitionSpec as P

MESH = pl.DeviceIdType.MESH
F32 = jnp.float32
BF16 = jnp.bfloat16

KLOC = 96
SLOT = 128
HALF = KLOC // 2
MOVE = 32
NX, NY, NZ = 4, 4, 16
BD = 256
DB = 1024
CW = 256
CAP = 512
NONE = -1.0e6
epsilon = 1e-05


def dot(a, b):
    return jnp.dot(a, b, preferred_element_type=F32)


def dot_nt(a, b):
    return lax.dot_general(a, b, (((1,), (1,)), ((), ())), preferred_element_type=F32)


def iota(shape, dim):
    return lax.broadcasted_iota(jnp.int32, shape, dim)


ORDER = (2, 1, 3, 0)


def kernel(
    bs_hbm, co_hbm, wu_in, wd_in, marks_hbm, oc_hbm,
    hid_hbm, gu_out, gd_out,
    bs, co, marks_in, oc_in, pw, rw, wur, wdr, wu, wd, xn, xc, nt, ct, hh, pg, ff,
    gu32, gub, gd32, gdb,
    ux, ua, ua2, ub, u1, u1b, u2b,
    dx, da, da2, db, d1, d1b, d2b,
    hs, hr, ho, hq, cx, cz, sb, rb, s0, r0,
    in_sem, out_sem,
    w_ss, w_rs,
    wuz_ss, wuz_rs, wua_ss, wua_rs, wux_ss, wux_rs,
    wdz_ss, wdz_rs, wda_ss, wda_rs, wdx_ss, wdx_rs,
    y_ss, y_rs, s_ss, s_rs,
    gux_ss, gux_rs, gua_ss, gua_rs, gub_ss, gub_rs,
    gdx_ss, gdx_rs, gda_ss, gda_rs, gdb_ss, gdb_rs,
    h_ss, h_rs, f_ss, f_rs, c_ss, c_rs,
):
    s = lax.axis_index("seq")
    t = lax.axis_index("tp")
    c = s % 2
    k = s // 2
    x = k % NX
    z = k // NX
    oc = 1 - c

    def at(zz, xx, cc, tt):
        return (((zz + NZ) % NZ * NX + (xx + NX) % NX) * 2 + cc, (tt + NY) % NY)

    sib = at(z, x, oc, t)
    yp, ym = at(z, x, c, t + 1), at(z, x, c, t - 1)
    xs = [at(z, x + 1, c, t), at(z, x - 1, c, t), at(z, x + 2, c, t)]
    z1p, z1m, z2p, z2m = (at(z + d, x, c, t) for d in (1, -1, 2, -2))
    z4p, z4m, z4p_other, z4m_other = (at(z + d, x, cc, t) for cc in (c, oc) for d in (4, -4))
    x_of = [(x + 1) % NX, (x + 3) % NX, (x + 2) % NX]
    nk = NZ * NX
    k_next = ((k + 1) % nk * 2 + c, t)
    k_prev = ((k + nk - 1) % nk * 2 + c, t)

    sends = []

    def send(src, dst, ss, rs, to):
        cp = pltpu.make_async_remote_copy(
            src_ref=src, dst_ref=dst, send_sem=ss, recv_sem=rs, device_id=to, device_id_type=MESH
        )
        cp.start()
        sends.append(cp)
        return cp

    peers = [sib, yp, ym] + xs + [z1p, z1m, z2p, z2m]
    peers += [z4p, z4m, z4p_other, z4m_other, k_next, k_prev]
    barrier = pltpu.get_barrier_semaphore()
    for p in peers:
        pl.semaphore_signal(barrier, inc=1, device_id=p, device_id_type=MESH)
    in_cps = [
        pltpu.make_async_copy(a, b, in_sem.at[i])
        for i, (a, b) in enumerate(
            ((marks_hbm, marks_in), (oc_hbm, oc_in), (bs_hbm, bs), (co_hbm, co))
        )
    ]
    for cp in in_cps:
        cp.start()
    in_cps[0].wait()

    marks = marks_in[...].astype(F32)
    row8 = iota((8, 128), 0)
    lane8 = iota((8, 128), 1)
    per_row = jnp.sum(marks, axis=1, keepdims=True)
    own_counts = jnp.sum(
        jnp.where(row8 // 2 + 4 * c == lane8, per_row, 0.0), axis=0, keepdims=True
    )
    counts16 = jnp.broadcast_to(own_counts, (16, 128)).astype(BF16)
    both_w = jnp.concatenate([wu_in[...].astype(F32), wd_in[...].astype(F32)], axis=0).astype(BF16)
    for h in range(2):
        pw[h, :, 0:CW] = both_w[:, h * CW : (h + 1) * CW]
        pw[h, :, CW : CW + 128] = counts16

    pl.semaphore_wait(barrier, len(peers))
    w_cp = send(pw.at[oc], rw, w_ss, w_rs, sib)

    own_marks = jnp.concatenate(
        [
            jnp.sum(jnp.where(row8 == 2 * t + h, marks, 0.0), axis=0, keepdims=True)
            for h in range(2)
        ],
        axis=1,
    )
    upto = (iota((BD, BD), 0) <= iota((BD, BD), 1)).astype(F32).astype(BF16)
    rank = dot(jnp.broadcast_to(own_marks, (16, BD)).astype(BF16), upto)[0:1]
    slot_ids = iota((KLOC, BD), 0).astype(F32)
    in_span = jnp.where(slot_ids == rank - 1.0, 1.0, 0.0)
    segment = in_span.astype(BF16)
    select = (in_span * own_marks).astype(BF16)

    in_cps[2].wait()
    picked = dot(select, bs[...])
    inverse_rms = lax.rsqrt(jnp.mean(picked * picked, axis=1, keepdims=True) + epsilon)
    xn[c, t] = (picked * inverse_rms).astype(BF16)

    def send_own(buf, kind):
        own = buf.at[c, t]
        return (
            send(own, own, y_ss.at[kind, 0], y_rs.at[kind, 0], yp),
            send(own, own, y_ss.at[kind, 1], y_rs.at[kind, 1], ym),
            send(own, own, s_ss.at[kind, 0], s_rs.at[kind, 0], sib),
        )

    own_n = send_own(xn, 0)
    in_cps[3].wait()
    xc[c, t] = dot(segment, co[...]).astype(BF16)
    own_c = send_own(xc, 1)

    tp_, tm_, t2_ = (t + 1) % NY, (t + NY - 1) % NY, (t + 2) % NY

    def forward(buf, kind, own):
        own[0].wait_recv()
        a = buf.at[c, tm_, 0:HALF]
        f0 = send(a, a, y_ss.at[kind, 2], y_rs.at[kind, 2], yp)
        a = buf.at[c, tm_]
        g0 = send(a, a, s_ss.at[kind, 1], s_rs.at[kind, 1], sib)
        own[1].wait_recv()
        a = buf.at[c, tp_, HALF:KLOC]
        f1 = send(a, a, y_ss.at[kind, 3], y_rs.at[kind, 3], ym)
        a = buf.at[c, tp_]
        g1 = send(a, a, s_ss.at[kind, 2], s_rs.at[kind, 2], sib)
        return f0, f1, g0, g1

    def forward_far(buf, kind, f):
        f[0].wait_recv()
        a = buf.at[c, t2_, 0:HALF]
        g2 = send(a, a, s_ss.at[kind, 3], s_rs.at[kind, 3], sib)
        f[1].wait_recv()
        a = buf.at[c, t2_, HALF:KLOC]
        g3 = send(a, a, s_ss.at[kind, 4], s_rs.at[kind, 4], sib)
        return g2, g3

    eye = (iota((256, 256), 0) == iota((256, 256), 1)).astype(F32).astype(BF16)
    filler = jnp.zeros((SLOT - KLOC, DB), BF16)

    def rows_of(buf, cc, tt):
        return jnp.concatenate([buf[cc, tt], filler], axis=0)

    def transpose(buf, out, cc, tt):
        rows = rows_of(buf, cc, tt)
        for j in range(DB // 256):
            out[cc * 4 + tt, j * 256 : (j + 1) * 256, :] = dot_nt(
                eye, rows[:, j * 256 : (j + 1) * 256]
            ).astype(BF16)

    def up(cc, tt):
        v = dot(rows_of(xn, cc, tt), wu[...])
        sg = jax.nn.sigmoid(v)
        hh[cc * 4 + tt] = (v * sg).astype(BF16)
        ff[cc * 4 + tt] = sg * (1.0 + v * (1.0 - sg))

    def back(cc, tt):
        v = dot(rows_of(xc, cc, tt), wd[...])
        pg[cc * 4 + tt] = (v * ff[cc * 4 + tt]).astype(BF16)

    def arrive(cps):
        for cp in cps:
            cp.wait_recv()

    w_cp.wait_recv()
    mine, other = pw[c].astype(F32), rw[...].astype(F32)
    low, high = jnp.where(c == 0, mine, other), jnp.where(c == 0, other, mine)
    wur[0, 1, x] = jnp.concatenate([low[0:8, 0:CW], high[0:8, 0:CW]], axis=0).astype(BF16)
    wdr[0, 1, x] = jnp.concatenate([low[8:16, 0:CW], high[8:16, 0:CW]], axis=0).astype(BF16)
    cx[x] = low[0:1, CW:] + high[0:1, CW:]

    def stride(src, dst, j, to):
        return [
            send(b.at[src, 1, x], b.at[dst, 1, x], ss.at[j], rs.at[j], to)
            for b, ss, rs in ((wur, wuz_ss, wuz_rs), (wdr, wdz_ss, wdz_rs))
        ]

    w_z = {3: stride(0, 3, 0, z4p), 1: stride(0, 1, 1, z4m)}
    c_x = [send(cx.at[x], cx.at[x], c_ss.at[j], c_rs.at[j], xs[j]) for j in range(3)]

    def spread_near(part, m, ss, rs):
        cps = {
            (m, 0): send(part(m, 1), part(m, 0), ss.at[0, m], rs.at[0, m], z1p),
            (m, 2): send(part(m, 1), part(m, 2), ss.at[1, m], rs.at[1, m], z1m),
        }
        for to, mm, j in ((z2p, {0: 3, 3: 2}, 2), (z2m, {0: 0, 1: 1}, 3)):
            if m in mm:
                cps[mm[m], 3] = send(part(m, 1), part(mm[m], 3), ss.at[j, m], rs.at[j, m], to)
        return cps

    def spread_x(a, m, ss, rs):
        return [send(a, a, ss.at[j, m], rs.at[j, m], xs[j]) for j in range(3)]

    near_u, near_d, side_u, side_d = {}, {}, {}, {}

    def first_step(m):
        if m:
            arrive(w_z[m])
            if m == 3:
                w_z[2] = stride(3, 2, 2, z4p)
        near_u.update(spread_near(lambda mm, e: wur.at[mm, e, x], m, wua_ss, wua_rs))
        side_d[m] = spread_x(wdr.at[m, 1, x], m, wdx_ss, wdx_rs)

    def second_step(m):
        arrive([near_u[m, e] for e in (0, 2, 3)])
        side_u[m] = spread_x(wur.at[m, :, x], m, wux_ss, wux_rs)
        arrive(side_d[m])
        near_d.update(spread_near(lambda mm, e: wdr.at[mm, e], m, wda_ss, wda_rs))

    def settle(buf, out):
        for m in range(4):
            for e in range(4):
                at_z = (z + 4 * m + e - 1 + NZ) % NZ
                out[pl.ds(pl.multiple_of(at_z * 64, 64), 64), :] = buf[m, e].reshape(64, out.shape[1])

    first_step(0)
    arrive(c_x)
    lane1 = iota((1, 128), 1)
    here = cx[x]
    at_z_total = jnp.sum(cx[0] + cx[1] + cx[2] + cx[3], axis=1, keepdims=True)
    cz[0, 1] = jnp.broadcast_to(at_z_total, (1, 128))
    c_z = [
        send(cz.at[0, 1], cz.at[3, 1], c_ss.at[3], c_rs.at[3], z4p),
        send(cz.at[0, 1], cz.at[1, 1], c_ss.at[4], c_rs.at[4], z4m),
    ]
    transpose(xn, nt, c, t)
    transpose(xc, ct, c, t)
    first_step(3)
    first_step(1)
    arrive(c_z)
    c_far = send(cz.at[3, 1], cz.at[2, 1], c_ss.at[5], c_rs.at[5], z4p)
    second_step(0)
    far_n = forward(xn, 0, own_n)
    first_step(2)
    c_far.wait_recv()
    c_near = [
        send(cz.at[:, 1], cz.at[:, 0], c_ss.at[6], c_rs.at[6], z1p),
        send(cz.at[:, 1], cz.at[:, 2], c_ss.at[7], c_rs.at[7], z1m),
    ] + [
        send(cz.at[a, 1], cz.at[b, 3], c_ss.at[j], c_rs.at[j], to)
        for j, a, b, to in ((8, 0, 3, z2p), (9, 3, 2, z2p), (10, 0, 0, z2m), (11, 1, 1, z2m))
    ]
    second_step(3)
    second_step(1)
    second_step(2)
    own_n[2].wait_recv()
    transpose(xn, nt, oc, t)
    transpose(xn, nt, c, tm_)
    transpose(xn, nt, c, tp_)

    far_c = forward(xc, 1, own_c)
    own_c[2].wait_recv()
    transpose(xc, ct, oc, t)
    transpose(xc, ct, c, tm_)
    transpose(xc, ct, c, tp_)
    far_n[2].wait_recv()
    far_n[3].wait_recv()
    transpose(xn, nt, oc, tm_)
    transpose(xn, nt, oc, tp_)

    last_n = forward_far(xn, 0, far_n)
    for m in range(4):
        arrive(side_u[m])
    settle(wur, wu)
    for cc, tt in ((c, t), (oc, t), (c, tm_), (c, tp_), (oc, tm_), (oc, tp_), (c, t2_)):
        up(cc, tt)
    transpose(xn, nt, c, t2_)
    last_c = forward_far(xc, 1, far_c)
    for m in range(4):
        arrive([near_d[m, e] for e in (0, 2, 3)])
    settle(wdr, wd)
    far_c[2].wait_recv()
    far_c[3].wait_recv()
    transpose(xc, ct, oc, tm_)
    transpose(xc, ct, oc, tp_)
    transpose(xc, ct, c, t2_)
    for cc, tt in ((c, t), (oc, t), (c, tm_), (c, tp_), (oc, tm_), (oc, tp_), (c, t2_)):
        back(cc, tt)
    last_n[0].wait_recv()
    last_n[1].wait_recv()
    up(oc, t2_)
    transpose(xn, nt, oc, t2_)
    arrive(c_near)
    before = jnp.zeros((1, 128), F32)
    for m in range(4):
        for e in range(4):
            before = before + jnp.where((z + 4 * m + e - 1 + NZ) % NZ < z, cz[m, e], 0.0)
    beside = jnp.zeros((1, 128), F32)
    for xx in range(NX):
        beside = beside + jnp.where(xx < x, cx[xx], 0.0)
    before_a = before[:, 0:1] + jnp.sum(beside, axis=1, keepdims=True)
    slot1 = lane1.astype(F32)
    pos, totals = [], []
    for g in range(2):
        first = jnp.zeros((1, 1), F32)
        parts = []
        for p in range(4):
            n = jnp.sum(jnp.where(lane1 == 4 * g + p, here, 0.0), axis=1, keepdims=True)
            parts.append(jnp.where(slot1 < n, slot1 + first, NONE))
            first = first + n
        pos.append(jnp.concatenate(parts, axis=1))
        totals.append(first)
    in_cps[1].wait()
    owners = oc_in[...].astype(F32)
    owner_first = jnp.sum(jnp.where(lane1 < 2 * k, owners, 0.0), axis=1, keepdims=True)
    owned = [
        jnp.sum(jnp.where(lane1 == 2 * k + g, owners, 0.0), axis=1, keepdims=True)
        for g in range(2)
    ]
    shift = [owner_first - before_a, owner_first + owned[0] - before_a - totals[0]]
    end_ids = iota((MOVE, CAP), 0).astype(F32)
    group_rows = [hh[4 * g : 4 * g + 4].reshape(CAP, CW) for g in range(2)]

    def ends(g, base):
        table = jnp.where(end_ids + base == pos[g], 1.0, 0.0).astype(BF16)
        return dot(table, group_rows[g]).astype(BF16)

    hs[0] = ends(0, 0.0)
    hs[1] = ends(1, totals[1] - MOVE)
    h_p = send(hs.at[0], hr.at[0], h_ss.at[0], h_rs.at[0], k_prev)
    h_n = send(hs.at[1], hr.at[1], h_ss.at[1], h_rs.at[1], k_next)
    first_b = ends(1, 0.0)
    last_a = ends(0, totals[0] - MOVE)

    row_ids = iota((CAP, CAP), 0).astype(F32)
    end_row = iota((CAP, 2 * MOVE), 0).astype(F32)
    end_lane1 = iota((1, 2 * MOVE), 1)
    end_at = end_lane1.astype(F32)

    def place(g, edge):
        inner = jnp.where(
            (row_ids + shift[g] == pos[g]) & (row_ids < owned[g]), 1.0, 0.0
        ).astype(BF16)
        end_pos = jnp.where(end_lane1 < MOVE, end_at - MOVE, end_at - MOVE + totals[g])
        outer = jnp.where(
            (end_row + shift[g] == end_pos) & (end_row < owned[g]), 1.0, 0.0
        ).astype(BF16)
        ho[g] = (dot(inner, group_rows[g]) + dot(outer, edge)).astype(BF16)


    last_c[0].wait_recv()
    last_c[1].wait_recv()
    transpose(xc, ct, oc, t2_)
    back(oc, t2_)

    def grad(m, left_ref, right_ref, g32, gb):
        rows = []
        for e in range(4):
            at_z = (z + 4 * m + e - 1 + NZ) % NZ
            part = pl.ds(pl.multiple_of(at_z * 64, 64), 64)
            rows.append(jnp.concatenate([left_ref[b, part, :] for b in range(8)], axis=1))
        r = dot(jnp.concatenate(rows, axis=0), right_ref[...].reshape(8 * SLOT, CW))
        r = r.reshape(4, NX, 16, CW)
        g32[m] = r
        gb[m] = r.astype(BF16)

    def near_sum(part, m, into, into2, ss, rs):
        to2 = z2p if m < 2 else z2m
        return [
            send(part(m, 2), into.at[0, m], ss.at[0, m], rs.at[0, m], z1p),
            send(part(m, 0), into.at[1, m], ss.at[1, m], rs.at[1, m], z1m),
            send(part(m, 3), into2.at[m], ss.at[2, m], rs.at[2, m], to2),
        ]

    def near_total(own, m, cps, into, into2):
        far = {0: (0, 3), 1: (1,), 2: (), 3: (2,)}[m]
        arrive(cps[m][0:2] + [cps[i][2] for i in far])
        r = own + into[0, m].astype(F32) + into[1, m].astype(F32)
        for i in far:
            r = r + into2[i].astype(F32)
        return r

    def side_total(own, m, cps, into):
        arrive(cps[m])
        return own + into[0, m].astype(F32) + into[1, m].astype(F32) + into[2, m].astype(F32)

    g_dn, g_ux, g_dx, g_un, part_d, part_u = {}, {}, {}, {}, {}, {}

    def start(m):
        grad(m, ct, hh, gd32, gdb)
        g_dn[m] = near_sum(lambda mm, e: gdb.at[mm, e], m, da, da2, gda_ss, gda_rs)
        grad(m, nt, pg, gu32, gub)
        g_ux[m] = [
            send(gub.at[m, :, x_of[j]], ux.at[j, m], gux_ss.at[j, m], gux_rs.at[j, m], xs[j])
            for j in range(3)
        ]

    def d_first(m):
        r = near_total(gd32[m, 1], m, g_dn, da, da2)
        d1[m] = r
        d1b[m] = r.astype(BF16)
        g_dx[m] = [
            send(d1b.at[m, x_of[j]], dx.at[j, m], gdx_ss.at[j, m], gdx_rs.at[j, m], xs[j])
            for j in range(3)
        ]

    def u_first(m):
        r = side_total(gu32[m, :, x], m, g_ux, ux)
        u1[m] = r
        u1b[m] = r.astype(BF16)
        g_un[m] = near_sum(lambda mm, e: u1b.at[mm, e], m, ua, ua2, gua_ss, gua_rs)

    def halves(m):
        return [
            jnp.concatenate([part_u[m][8 * h : 8 * h + 8], part_d[m][8 * h : 8 * h + 8]], axis=0)
            for h in range(2)
        ]

    g_far, g_end = [], {}

    def both_second(m):
        part_d[m] = side_total(d1[m, x], m, g_dx, dx)
        part_u[m] = near_total(u1[m, 1], m, g_un, ua, ua2)
        if m == 2:
            u2b[...] = part_u[m].astype(BF16)
            d2b[...] = part_d[m].astype(BF16)
            g_far.append(send(u2b, ub, gub_ss.at[0], gub_rs.at[0], z4p))
            g_far.append(send(d2b, db, gdb_ss.at[0], gdb_rs.at[0], z4p))
            return
        if m == 1:
            arrive(g_far)
            part_u[m] = part_u[m] + ub[...].astype(F32)
            part_d[m] = part_d[m] + db[...].astype(F32)
        h = halves(m)
        if m == 0:
            s0[0], s0[1] = h
            g_end[m] = [send(s0.at[oc], r0, f_ss, f_rs, sib)]
            return
        slot = {1: 0, 3: 1}[m]
        sb[slot, 0] = h[0].astype(BF16)
        sb[slot, 1] = h[1].astype(BF16)
        same, other = {1: (z4p, z4p_other), 3: (z4m, z4m_other)}[m]
        g_end[m] = [
            send(sb.at[slot, c], rb.at[slot, c], gub_ss.at[m], gub_rs.at[m], same),
            send(sb.at[slot, oc], rb.at[slot, c], gdb_ss.at[m], gdb_rs.at[m], other),
        ]

    def both_first(m):
        d_first(m)
        u_first(m)

    start(2)
    start(1)
    both_first(2)
    start(3)
    both_first(1)
    both_second(2)
    start(0)

    h_p.wait_recv()
    h_n.wait_recv()
    place(0, jnp.concatenate([hr[1], first_b], axis=0))
    place(1, jnp.concatenate([last_a, hr[0]], axis=0))
    h_s = send(ho.at[oc], hq, h_ss.at[2], h_rs.at[2], sib)
    out_own = pltpu.make_async_copy(
        ho.at[c], hid_hbm.at[:, pl.ds(pl.multiple_of(c * CW, CW), CW)], out_sem.at[0]
    )
    out_own.start()

    both_first(3)
    both_second(1)
    both_first(0)
    both_second(3)
    both_second(0)

    h_s.wait_recv()
    out_sib = pltpu.make_async_copy(
        hq, hid_hbm.at[:, pl.ds(pl.multiple_of(oc * CW, CW), CW)], out_sem.at[1]
    )
    out_sib.start()

    arrive(g_end[1] + g_end[3] + g_end[0])
    mine = s0[c] + rb[0, c].astype(F32) + rb[1, c].astype(F32)
    other = r0[...] + rb[0, oc].astype(F32) + rb[1, oc].astype(F32)
    low, high = jnp.where(c == 0, mine, other), jnp.where(c == 0, other, mine)
    for i, out in enumerate((gu_out, gd_out)):
        out[:, 0:CW] = low[8 * i : 8 * i + 8]
        out[:, CW:] = high[8 * i : 8 * i + 8]

    for cp in sends:
        cp.wait_send()
    out_own.wait()
    out_sib.wait()


def body(byte_states, cotangent, w_up, w_down, bounds, owner_counts):
    vmem = pl.BlockSpec(memory_space=pltpu.VMEM)
    hbm = pl.BlockSpec(memory_space=pltpu.HBM)
    dma = pltpu.SemaphoreType.DMA
    parts = (4, 4, NX, 16, CW)
    scratch = [
        pltpu.VMEM((BD, DB), BF16),
        pltpu.VMEM((BD, DB), BF16),
        pltpu.VMEM((8, 128), jnp.int32),
        pltpu.VMEM((1, 128), jnp.int32),
        pltpu.VMEM((2, 16, CW + 128), BF16),
        pltpu.VMEM((16, CW + 128), BF16),
        pltpu.VMEM(parts, BF16),
        pltpu.VMEM(parts, BF16),
        pltpu.VMEM((DB, CW), BF16),
        pltpu.VMEM((DB, CW), BF16),
        pltpu.VMEM((2, NY, KLOC, DB), BF16),
        pltpu.VMEM((2, NY, KLOC, DB), BF16),
        pltpu.VMEM((8, DB, SLOT), BF16),
        pltpu.VMEM((8, DB, SLOT), BF16),
        pltpu.VMEM((8, SLOT, CW), BF16),
        pltpu.VMEM((8, SLOT, CW), BF16),
        pltpu.VMEM((8, SLOT, CW), F32),
        pltpu.VMEM(parts, F32),
        pltpu.VMEM(parts, BF16),
        pltpu.VMEM(parts, F32),
        pltpu.VMEM(parts, BF16),
        pltpu.VMEM((3, 4, 4, 16, CW), BF16),
        pltpu.VMEM((2, 4, 16, CW), BF16),
        pltpu.VMEM((4, 16, CW), BF16),
        pltpu.VMEM((16, CW), BF16),
        pltpu.VMEM((4, 4, 16, CW), F32),
        pltpu.VMEM((4, 4, 16, CW), BF16),
        pltpu.VMEM((16, CW), BF16),
        pltpu.VMEM((3, 4, 16, CW), BF16),
        pltpu.VMEM((2, 4, NX, 16, CW), BF16),
        pltpu.VMEM((4, NX, 16, CW), BF16),
        pltpu.VMEM((16, CW), BF16),
        pltpu.VMEM((4, NX, 16, CW), F32),
        pltpu.VMEM((4, NX, 16, CW), BF16),
        pltpu.VMEM((16, CW), BF16),
        pltpu.VMEM((2, MOVE, CW), BF16),
        pltpu.VMEM((2, MOVE, CW), BF16),
        pltpu.VMEM((2, CAP, CW), BF16),
        pltpu.VMEM((CAP, CW), BF16),
        pltpu.VMEM((NX, 1, 128), F32),
        pltpu.VMEM((4, 4, 1, 128), F32),
        pltpu.VMEM((2, 2, 16, CW), BF16),
        pltpu.VMEM((2, 2, 16, CW), BF16),
        pltpu.VMEM((2, 16, CW), F32),
        pltpu.VMEM((16, CW), F32),
        dma((4,)),
        dma((2,)),
        dma, dma,
        dma((3,)), dma((3,)), dma((4, 4)), dma((4, 4)), dma((3, 4)), dma((3, 4)),
        dma((3,)), dma((3,)), dma((4, 4)), dma((4, 4)), dma((3, 4)), dma((3, 4)),
        dma((2, 4)), dma((2, 4)), dma((2, 5)), dma((2, 5)),
        dma((3, 4)), dma((3, 4)), dma((3, 4)), dma((3, 4)), dma((4,)), dma((4,)),
        dma((3, 4)), dma((3, 4)), dma((3, 4)), dma((3, 4)), dma((4,)), dma((4,)),
        dma((3,)), dma((3,)), dma, dma,
        dma((12,)), dma((12,)),
    ]
    hidden, grad_up, grad_down = pl.pallas_call(
        kernel,
        out_shape=(
            jax.ShapeDtypeStruct((CAP, 2 * CW), BF16),
            jax.ShapeDtypeStruct((8, 2 * CW), F32),
            jax.ShapeDtypeStruct((8, 2 * CW), F32),
        ),
        in_specs=[hbm, hbm, vmem, vmem, hbm, hbm],
        out_specs=(hbm, vmem, vmem),
        scratch_shapes=scratch,
        compiler_params=pltpu.CompilerParams(
            collective_id=0, has_side_effects=True, vmem_limit_bytes=48 * 1024 * 1024
        ),
        cost_estimate=pl.CostEstimate(
            flops=4 * 10**9, bytes_accessed=2 * 1024 * 1024, transcendentals=262144
        ),
    )(
        *(
            pltpu.with_memory_space_constraint(a, pltpu.HBM)
            for a in (
                byte_states,
                cotangent,
                w_up,
                w_down.T,
                bounds.reshape(8, 128),
                owner_counts.reshape(1, 128),
            )
        )
    )
    return hidden, grad_up, grad_down.T


def solution(mesh):
    return jax.shard_map(
        body,
        mesh=mesh,
        in_specs=(
            P(("seq", "tp"), None),
            P(("seq", "tp"), None),
            P("seq", "tp"),
            P("tp", "seq"),
            P("seq"),
            P(),
        ),
        out_specs=(P("seq", "tp"), P("seq", "tp"), P("tp", "seq")),
        check_vma=False,
    )
```

```python
import functools

import jax
import jax.numpy as jnp
from jax import lax
from jax.experimental import pallas as pl
from jax.experimental.pallas import tpu as pltpu
from jax.sharding import PartitionSpec as P

MESH = pl.DeviceIdType.MESH
F32 = jnp.float32
BF16 = jnp.bfloat16

KLOC = 96
SLOT = 128
HALF = KLOC // 2
MOVE = 32
NX, NY, NZ = 4, 4, 16
BD = 256
DB = 1024
CW = 256
CAP = 512
NONE = -1.0e6
epsilon = 1e-05


def dot(a, b):
    return jnp.dot(a, b, preferred_element_type=F32)


def dot_nt(a, b):
    return lax.dot_general(a, b, (((1,), (1,)), ((), ())), preferred_element_type=F32)


def iota(shape, dim):
    return lax.broadcasted_iota(jnp.int32, shape, dim)


ORDER = (2, 1, 3, 0)


def kernel(
    bs_hbm, co_hbm, wu_hbm, wd_hbm, marks_hbm, oc_hbm,
    hid_hbm, gu_out, gd_out,
    bs, co, marks_in, oc_in, wu_in, wd_in, pw, rw, wur, wdr, wu, wd, xn, xc, nt, ct, hh, pg, ff,
    gu32, gub, gd32, gdb,
    ux, ua, ua2, ub, u1, u1b, u2b,
    dx, da, da2, db, d1, d1b, d2b,
    hs, hr, ho, hq, cx, cz, sb, rb, s0, r0,
    in_sem, out_sem,
    w_ss, w_rs,
    wuz_ss, wuz_rs, wua_ss, wua_rs, wux_ss, wux_rs,
    wdz_ss, wdz_rs, wda_ss, wda_rs, wdx_ss, wdx_rs,
    y_ss, y_rs, s_ss, s_rs,
    gux_ss, gux_rs, gua_ss, gua_rs, gub_ss, gub_rs,
    gdx_ss, gdx_rs, gda_ss, gda_rs, gdb_ss, gdb_rs,
    h_ss, h_rs, f_ss, f_rs, c_ss, c_rs,
):
    s = lax.axis_index("seq")
    t = lax.axis_index("tp")
    c = s % 2
    k = s // 2
    x = k % NX
    z = k // NX
    oc = 1 - c

    def at(zz, xx, cc, tt):
        return (((zz + NZ) % NZ * NX + (xx + NX) % NX) * 2 + cc, (tt + NY) % NY)

    sib = at(z, x, oc, t)
    yp, ym = at(z, x, c, t + 1), at(z, x, c, t - 1)
    xs = [at(z, x + 1, c, t), at(z, x - 1, c, t), at(z, x + 2, c, t)]
    z1p, z1m, z2p, z2m = (at(z + d, x, c, t) for d in (1, -1, 2, -2))
    z4p, z4m, z4p_other, z4m_other = (at(z + d, x, cc, t) for cc in (c, oc) for d in (4, -4))
    x_of = [(x + 1) % NX, (x + 3) % NX, (x + 2) % NX]
    nk = NZ * NX
    k_next = ((k + 1) % nk * 2 + c, t)
    k_prev = ((k + nk - 1) % nk * 2 + c, t)

    sends = []

    def send(src, dst, ss, rs, to):
        cp = pltpu.make_async_remote_copy(
            src_ref=src, dst_ref=dst, send_sem=ss, recv_sem=rs, device_id=to, device_id_type=MESH
        )
        cp.start()
        sends.append(cp)
        return cp

    peers = [sib, yp, ym] + xs + [z1p, z1m, z2p, z2m]
    peers += [z4p, z4m, z4p_other, z4m_other, k_next, k_prev]
    barrier = pltpu.get_barrier_semaphore()
    for p in peers:
        pl.semaphore_signal(barrier, inc=1, device_id=p, device_id_type=MESH)
    in_cps = [
        pltpu.make_async_copy(a, b, in_sem.at[i])
        for i, (a, b) in enumerate(
            (
                (marks_hbm, marks_in),
                (oc_hbm, oc_in),
                (bs_hbm, bs),
                (co_hbm, co),
                (wu_hbm, wu_in),
                (wd_hbm, wd_in),
            )
        )
    ]
    for cp in in_cps:
        cp.start()
    for i in (0, 4, 5):
        in_cps[i].wait()

    marks = marks_in[...].astype(F32)
    row8 = iota((8, 128), 0)
    lane8 = iota((8, 128), 1)
    per_row = jnp.sum(marks, axis=1, keepdims=True)
    own_counts = jnp.sum(
        jnp.where(row8 // 2 + 4 * c == lane8, per_row, 0.0), axis=0, keepdims=True
    )
    counts16 = jnp.broadcast_to(own_counts, (16, 128)).astype(BF16)
    both_w = jnp.concatenate([wu_in[...].astype(F32), wd_in[...].astype(F32)], axis=0).astype(BF16)
    for h in range(2):
        pw[h, :, 0:CW] = both_w[:, h * CW : (h + 1) * CW]
        pw[h, :, CW : CW + 128] = counts16

    pl.semaphore_wait(barrier, len(peers))
    w_cp = send(pw.at[oc], rw, w_ss, w_rs, sib)

    own_marks = jnp.concatenate(
        [
            jnp.sum(jnp.where(row8 == 2 * t + h, marks, 0.0), axis=0, keepdims=True)
            for h in range(2)
        ],
        axis=1,
    )
    upto = (iota((BD, BD), 0) <= iota((BD, BD), 1)).astype(F32).astype(BF16)
    rank = dot(jnp.broadcast_to(own_marks, (16, BD)).astype(BF16), upto)[0:1]
    slot_ids = iota((KLOC, BD), 0).astype(F32)
    in_span = jnp.where(slot_ids == rank - 1.0, 1.0, 0.0)
    segment = in_span.astype(BF16)
    select = (in_span * own_marks).astype(BF16)

    in_cps[2].wait()
    picked = dot(select, bs[...])
    inverse_rms = lax.rsqrt(jnp.mean(picked * picked, axis=1, keepdims=True) + epsilon)
    xn[c, t] = (picked * inverse_rms).astype(BF16)

    def send_own(buf, kind):
        own = buf.at[c, t]
        return (
            send(own, own, y_ss.at[kind, 0], y_rs.at[kind, 0], yp),
            send(own, own, y_ss.at[kind, 1], y_rs.at[kind, 1], ym),
            send(own, own, s_ss.at[kind, 0], s_rs.at[kind, 0], sib),
        )

    own_n = send_own(xn, 0)
    in_cps[3].wait()
    xc[c, t] = dot(segment, co[...]).astype(BF16)
    own_c = send_own(xc, 1)

    tp_, tm_, t2_ = (t + 1) % NY, (t + NY - 1) % NY, (t + 2) % NY

    def forward(buf, kind, own):
        own[0].wait_recv()
        a = buf.at[c, tm_, 0:HALF]
        f0 = send(a, a, y_ss.at[kind, 2], y_rs.at[kind, 2], yp)
        a = buf.at[c, tm_]
        g0 = send(a, a, s_ss.at[kind, 1], s_rs.at[kind, 1], sib)
        own[1].wait_recv()
        a = buf.at[c, tp_, HALF:KLOC]
        f1 = send(a, a, y_ss.at[kind, 3], y_rs.at[kind, 3], ym)
        a = buf.at[c, tp_]
        g1 = send(a, a, s_ss.at[kind, 2], s_rs.at[kind, 2], sib)
        return f0, f1, g0, g1

    def forward_far(buf, kind, f):
        f[0].wait_recv()
        a = buf.at[c, t2_, 0:HALF]
        g2 = send(a, a, s_ss.at[kind, 3], s_rs.at[kind, 3], sib)
        f[1].wait_recv()
        a = buf.at[c, t2_, HALF:KLOC]
        g3 = send(a, a, s_ss.at[kind, 4], s_rs.at[kind, 4], sib)
        return g2, g3

    eye = (iota((256, 256), 0) == iota((256, 256), 1)).astype(F32).astype(BF16)
    filler = jnp.zeros((SLOT - KLOC, DB), BF16)

    def rows_of(buf, cc, tt):
        return jnp.concatenate([buf[cc, tt], filler], axis=0)

    def transpose(buf, out, cc, tt):
        rows = rows_of(buf, cc, tt)
        for j in range(DB // 256):
            out[cc * 4 + tt, j * 256 : (j + 1) * 256, :] = dot_nt(
                eye, rows[:, j * 256 : (j + 1) * 256]
            ).astype(BF16)

    hh[:, KLOC:, :] = jnp.zeros((8, SLOT - KLOC, CW), BF16)
    pg[:, KLOC:, :] = jnp.zeros((8, SLOT - KLOC, CW), BF16)

    def up(cc):
        v = dot(xn[cc].reshape(NY * KLOC, DB), wu[...])
        sg = jax.nn.sigmoid(v)
        hh[pl.ds(cc * 4, 4), 0:KLOC, :] = (v * sg).astype(BF16).reshape(NY, KLOC, CW)
        ff[cc] = sg * (1.0 + v * (1.0 - sg))

    def back(cc):
        v = dot(xc[cc].reshape(NY * KLOC, DB), wd[...])
        pg[pl.ds(cc * 4, 4), 0:KLOC, :] = (v * ff[cc]).astype(BF16).reshape(NY, KLOC, CW)

    def arrive(cps):
        for cp in cps:
            cp.wait_recv()

    w_cp.wait_recv()
    mine, other = pw[c].astype(F32), rw[...].astype(F32)
    low, high = jnp.where(c == 0, mine, other), jnp.where(c == 0, other, mine)
    wur[0, 1, x] = jnp.concatenate([low[0:8, 0:CW], high[0:8, 0:CW]], axis=0).astype(BF16)
    wdr[0, 1, x] = jnp.concatenate([low[8:16, 0:CW], high[8:16, 0:CW]], axis=0).astype(BF16)
    cx[x] = low[0:1, CW:] + high[0:1, CW:]

    def stride(src, dst, j, to):
        return [
            send(b.at[src, 1, x], b.at[dst, 1, x], ss.at[j], rs.at[j], to)
            for b, ss, rs in ((wur, wuz_ss, wuz_rs), (wdr, wdz_ss, wdz_rs))
        ]

    w_z = {3: stride(0, 3, 0, z4p), 1: stride(0, 1, 1, z4m)}
    c_x = [send(cx.at[x], cx.at[x], c_ss.at[j], c_rs.at[j], xs[j]) for j in range(3)]

    def spread_near(part, m, ss, rs):
        cps = {
            (m, 0): send(part(m, 1), part(m, 0), ss.at[0, m], rs.at[0, m], z1p),
            (m, 2): send(part(m, 1), part(m, 2), ss.at[1, m], rs.at[1, m], z1m),
        }
        for to, mm, j in ((z2p, {0: 3, 3: 2}, 2), (z2m, {0: 0, 1: 1}, 3)):
            if m in mm:
                cps[mm[m], 3] = send(part(m, 1), part(mm[m], 3), ss.at[j, m], rs.at[j, m], to)
        return cps

    def spread_x(a, m, ss, rs):
        return [send(a, a, ss.at[j, m], rs.at[j, m], xs[j]) for j in range(3)]

    near_u, near_d, side_u, side_d = {}, {}, {}, {}

    def first_step(m):
        if m:
            arrive(w_z[m])
            if m == 3:
                w_z[2] = stride(3, 2, 2, z4p)
        near_u.update(spread_near(lambda mm, e: wur.at[mm, e, x], m, wua_ss, wua_rs))
        side_d[m] = spread_x(wdr.at[m, 1, x], m, wdx_ss, wdx_rs)

    def second_step(m):
        arrive([near_u[m, e] for e in (0, 2, 3)])
        side_u[m] = spread_x(wur.at[m, :, x], m, wux_ss, wux_rs)
        arrive(side_d[m])
        near_d.update(spread_near(lambda mm, e: wdr.at[mm, e], m, wda_ss, wda_rs))

    def settle(buf, out):
        for m in range(4):
            for e in range(4):
                at_z = (z + 4 * m + e - 1 + NZ) % NZ
                out[pl.ds(pl.multiple_of(at_z * 64, 64), 64), :] = buf[m, e].reshape(64, out.shape[1])

    first_step(0)
    arrive(c_x)
    lane1 = iota((1, 128), 1)
    here = cx[x]
    at_z_total = jnp.sum(cx[0] + cx[1] + cx[2] + cx[3], axis=1, keepdims=True)
    cz[0, 1] = jnp.broadcast_to(at_z_total, (1, 128))
    c_z = [
        send(cz.at[0, 1], cz.at[3, 1], c_ss.at[3], c_rs.at[3], z4p),
        send(cz.at[0, 1], cz.at[1, 1], c_ss.at[4], c_rs.at[4], z4m),
    ]
    transpose(xn, nt, c, t)
    transpose(xc, ct, c, t)
    first_step(3)
    first_step(1)
    arrive(c_z)
    c_far = send(cz.at[3, 1], cz.at[2, 1], c_ss.at[5], c_rs.at[5], z4p)
    second_step(0)
    far_n = forward(xn, 0, own_n)
    first_step(2)
    c_far.wait_recv()
    c_near = [
        send(cz.at[:, 1], cz.at[:, 0], c_ss.at[6], c_rs.at[6], z1p),
        send(cz.at[:, 1], cz.at[:, 2], c_ss.at[7], c_rs.at[7], z1m),
    ] + [
        send(cz.at[a, 1], cz.at[b, 3], c_ss.at[j], c_rs.at[j], to)
        for j, a, b, to in ((8, 0, 3, z2p), (9, 3, 2, z2p), (10, 0, 0, z2m), (11, 1, 1, z2m))
    ]
    second_step(3)
    second_step(1)
    second_step(2)
    own_n[2].wait_recv()
    transpose(xn, nt, oc, t)
    transpose(xn, nt, c, tm_)
    transpose(xn, nt, c, tp_)

    far_c = forward(xc, 1, own_c)
    own_c[2].wait_recv()
    transpose(xc, ct, oc, t)
    transpose(xc, ct, c, tm_)
    transpose(xc, ct, c, tp_)
    far_n[2].wait_recv()
    far_n[3].wait_recv()
    transpose(xn, nt, oc, tm_)
    transpose(xn, nt, oc, tp_)

    last_n = forward_far(xn, 0, far_n)
    transpose(xn, nt, c, t2_)
    last_c = forward_far(xc, 1, far_c)
    far_c[2].wait_recv()
    far_c[3].wait_recv()
    transpose(xc, ct, oc, tm_)
    transpose(xc, ct, oc, tp_)
    last_n[0].wait_recv()
    last_n[1].wait_recv()
    transpose(xn, nt, oc, t2_)
    for m in range(4):
        arrive(side_u[m])
    settle(wur, wu)
    up(c)
    up(oc)
    transpose(xc, ct, c, t2_)
    for m in range(4):
        arrive([near_d[m, e] for e in (0, 2, 3)])
    settle(wdr, wd)
    back(c)

    arrive(c_near)
    before = jnp.zeros((1, 128), F32)
    for m in range(4):
        for e in range(4):
            before = before + jnp.where((z + 4 * m + e - 1 + NZ) % NZ < z, cz[m, e], 0.0)
    beside = jnp.zeros((1, 128), F32)
    for xx in range(NX):
        beside = beside + jnp.where(xx < x, cx[xx], 0.0)
    before_a = before[:, 0:1] + jnp.sum(beside, axis=1, keepdims=True)
    slot1 = lane1.astype(F32)
    pos, totals = [], []
    for g in range(2):
        first = jnp.zeros((1, 1), F32)
        parts = []
        for p in range(4):
            n = jnp.sum(jnp.where(lane1 == 4 * g + p, here, 0.0), axis=1, keepdims=True)
            parts.append(jnp.where(slot1 < n, slot1 + first, NONE))
            first = first + n
        pos.append(jnp.concatenate(parts, axis=1))
        totals.append(first)
    in_cps[1].wait()
    owners = oc_in[...].astype(F32)
    owner_first = jnp.sum(jnp.where(lane1 < 2 * k, owners, 0.0), axis=1, keepdims=True)
    owned = [
        jnp.sum(jnp.where(lane1 == 2 * k + g, owners, 0.0), axis=1, keepdims=True)
        for g in range(2)
    ]
    shift = [owner_first - before_a, owner_first + owned[0] - before_a - totals[0]]
    end_ids = iota((MOVE, CAP), 0).astype(F32)
    group_rows = [hh[4 * g : 4 * g + 4].reshape(CAP, CW) for g in range(2)]

    def ends(g, base):
        table = jnp.where(end_ids + base == pos[g], 1.0, 0.0).astype(BF16)
        return dot(table, group_rows[g]).astype(BF16)

    hs[0] = ends(0, 0.0)
    hs[1] = ends(1, totals[1] - MOVE)
    h_p = send(hs.at[0], hr.at[0], h_ss.at[0], h_rs.at[0], k_prev)
    h_n = send(hs.at[1], hr.at[1], h_ss.at[1], h_rs.at[1], k_next)
    first_b = ends(1, 0.0)
    last_a = ends(0, totals[0] - MOVE)

    row_ids = iota((CAP, CAP), 0).astype(F32)
    end_row = iota((CAP, 2 * MOVE), 0).astype(F32)
    end_lane1 = iota((1, 2 * MOVE), 1)
    end_at = end_lane1.astype(F32)

    def place(g, edge):
        inner = jnp.where(
            (row_ids + shift[g] == pos[g]) & (row_ids < owned[g]), 1.0, 0.0
        ).astype(BF16)
        end_pos = jnp.where(end_lane1 < MOVE, end_at - MOVE, end_at - MOVE + totals[g])
        outer = jnp.where(
            (end_row + shift[g] == end_pos) & (end_row < owned[g]), 1.0, 0.0
        ).astype(BF16)
        ho[g] = (dot(inner, group_rows[g]) + dot(outer, edge)).astype(BF16)


    last_c[0].wait_recv()
    last_c[1].wait_recv()
    transpose(xc, ct, oc, t2_)
    back(oc)

    def grad(m, left_ref, right_ref, g32, gb):
        rows = []
        for e in range(4):
            at_z = (z + 4 * m + e - 1 + NZ) % NZ
            part = pl.ds(pl.multiple_of(at_z * 64, 64), 64)
            rows.append(jnp.concatenate([left_ref[b, part, :] for b in range(8)], axis=1))
        r = dot(jnp.concatenate(rows, axis=0), right_ref[...].reshape(8 * SLOT, CW))
        r = r.reshape(4, NX, 16, CW)
        g32[m] = r
        gb[m] = r.astype(BF16)

    def near_sum(part, m, into, into2, ss, rs):
        to2 = z2p if m < 2 else z2m
        return [
            send(part(m, 2), into.at[0, m], ss.at[0, m], rs.at[0, m], z1p),
            send(part(m, 0), into.at[1, m], ss.at[1, m], rs.at[1, m], z1m),
            send(part(m, 3), into2.at[m], ss.at[2, m], rs.at[2, m], to2),
        ]

    def near_total(own, m, cps, into, into2):
        far = {0: (0, 3), 1: (1,), 2: (), 3: (2,)}[m]
        arrive(cps[m][0:2] + [cps[i][2] for i in far])
        r = own + into[0, m].astype(F32) + into[1, m].astype(F32)
        for i in far:
            r = r + into2[i].astype(F32)
        return r

    def side_total(own, m, cps, into):
        arrive(cps[m])
        return own + into[0, m].astype(F32) + into[1, m].astype(F32) + into[2, m].astype(F32)

    g_dn, g_ux, g_dx, g_un, part_d, part_u = {}, {}, {}, {}, {}, {}

    def start(m):
        grad(m, ct, hh, gd32, gdb)
        g_dn[m] = near_sum(lambda mm, e: gdb.at[mm, e], m, da, da2, gda_ss, gda_rs)
        grad(m, nt, pg, gu32, gub)
        g_ux[m] = [
            send(gub.at[m, :, x_of[j]], ux.at[j, m], gux_ss.at[j, m], gux_rs.at[j, m], xs[j])
            for j in range(3)
        ]

    def d_first(m):
        r = near_total(gd32[m, 1], m, g_dn, da, da2)
        d1[m] = r
        d1b[m] = r.astype(BF16)
        g_dx[m] = [
            send(d1b.at[m, x_of[j]], dx.at[j, m], gdx_ss.at[j, m], gdx_rs.at[j, m], xs[j])
            for j in range(3)
        ]

    def u_first(m):
        r = side_total(gu32[m, :, x], m, g_ux, ux)
        u1[m] = r
        u1b[m] = r.astype(BF16)
        g_un[m] = near_sum(lambda mm, e: u1b.at[mm, e], m, ua, ua2, gua_ss, gua_rs)

    def halves(m):
        return [
            jnp.concatenate([part_u[m][8 * h : 8 * h + 8], part_d[m][8 * h : 8 * h + 8]], axis=0)
            for h in range(2)
        ]

    g_far, g_end = [], {}

    def both_second(m):
        part_d[m] = side_total(d1[m, x], m, g_dx, dx)
        part_u[m] = near_total(u1[m, 1], m, g_un, ua, ua2)
        if m == 2:
            u2b[...] = part_u[m].astype(BF16)
            d2b[...] = part_d[m].astype(BF16)
            g_far.append(send(u2b, ub, gub_ss.at[0], gub_rs.at[0], z4p))
            g_far.append(send(d2b, db, gdb_ss.at[0], gdb_rs.at[0], z4p))
            return
        if m == 1:
            arrive(g_far)
            part_u[m] = part_u[m] + ub[...].astype(F32)
            part_d[m] = part_d[m] + db[...].astype(F32)
        h = halves(m)
        if m == 0:
            s0[0], s0[1] = h
            g_end[m] = [send(s0.at[oc], r0, f_ss, f_rs, sib)]
            return
        slot = {1: 0, 3: 1}[m]
        sb[slot, 0] = h[0].astype(BF16)
        sb[slot, 1] = h[1].astype(BF16)
        same, other = {1: (z4p, z4p_other), 3: (z4m, z4m_other)}[m]
        g_end[m] = [
            send(sb.at[slot, c], rb.at[slot, c], gub_ss.at[m], gub_rs.at[m], same),
            send(sb.at[slot, oc], rb.at[slot, c], gdb_ss.at[m], gdb_rs.at[m], other),
        ]

    def both_first(m):
        d_first(m)
        u_first(m)

    start(2)
    start(1)
    both_first(2)
    start(3)
    start(0)
    both_first(1)
    both_second(2)

    h_p.wait_recv()
    h_n.wait_recv()
    place(0, jnp.concatenate([hr[1], first_b], axis=0))
    place(1, jnp.concatenate([last_a, hr[0]], axis=0))
    h_s = send(ho.at[oc], hq, h_ss.at[2], h_rs.at[2], sib)
    out_own = pltpu.make_async_copy(
        ho.at[c], hid_hbm.at[:, pl.ds(pl.multiple_of(c * CW, CW), CW)], out_sem.at[0]
    )
    out_own.start()

    both_first(3)
    both_second(1)
    both_first(0)
    both_second(3)
    both_second(0)

    h_s.wait_recv()
    out_sib = pltpu.make_async_copy(
        hq, hid_hbm.at[:, pl.ds(pl.multiple_of(oc * CW, CW), CW)], out_sem.at[1]
    )
    out_sib.start()

    arrive(g_end[1] + g_end[3] + g_end[0])
    mine = s0[c] + rb[0, c].astype(F32) + rb[1, c].astype(F32)
    other = r0[...] + rb[0, oc].astype(F32) + rb[1, oc].astype(F32)
    low, high = jnp.where(c == 0, mine, other), jnp.where(c == 0, other, mine)
    for i, out in enumerate((gu_out, gd_out)):
        out[:, 0:CW] = low[8 * i : 8 * i + 8]
        out[:, CW:] = high[8 * i : 8 * i + 8]

    for cp in sends:
        cp.wait_send()
    out_own.wait()
    out_sib.wait()


def body(byte_states, cotangent, w_up, w_down, bounds, owner_counts):
    vmem = pl.BlockSpec(memory_space=pltpu.VMEM)
    hbm = pl.BlockSpec(memory_space=pltpu.HBM)
    dma = pltpu.SemaphoreType.DMA
    parts = (4, 4, NX, 16, CW)
    scratch = [
        pltpu.VMEM((BD, DB), BF16),
        pltpu.VMEM((BD, DB), BF16),
        pltpu.VMEM((8, 128), jnp.int32),
        pltpu.VMEM((1, 128), jnp.int32),
        pltpu.VMEM((8, 2 * CW), BF16),
        pltpu.VMEM((8, 2 * CW), BF16),
        pltpu.VMEM((2, 16, CW + 128), BF16),
        pltpu.VMEM((16, CW + 128), BF16),
        pltpu.VMEM(parts, BF16),
        pltpu.VMEM(parts, BF16),
        pltpu.VMEM((DB, CW), BF16),
        pltpu.VMEM((DB, CW), BF16),
        pltpu.VMEM((2, NY, KLOC, DB), BF16),
        pltpu.VMEM((2, NY, KLOC, DB), BF16),
        pltpu.VMEM((8, DB, SLOT), BF16),
        pltpu.VMEM((8, DB, SLOT), BF16),
        pltpu.VMEM((8, SLOT, CW), BF16),
        pltpu.VMEM((8, SLOT, CW), BF16),
        pltpu.VMEM((2, NY * KLOC, CW), F32),
        pltpu.VMEM(parts, F32),
        pltpu.VMEM(parts, BF16),
        pltpu.VMEM(parts, F32),
        pltpu.VMEM(parts, BF16),
        pltpu.VMEM((3, 4, 4, 16, CW), BF16),
        pltpu.VMEM((2, 4, 16, CW), BF16),
        pltpu.VMEM((4, 16, CW), BF16),
        pltpu.VMEM((16, CW), BF16),
        pltpu.VMEM((4, 4, 16, CW), F32),
        pltpu.VMEM((4, 4, 16, CW), BF16),
        pltpu.VMEM((16, CW), BF16),
        pltpu.VMEM((3, 4, 16, CW), BF16),
        pltpu.VMEM((2, 4, NX, 16, CW), BF16),
        pltpu.VMEM((4, NX, 16, CW), BF16),
        pltpu.VMEM((16, CW), BF16),
        pltpu.VMEM((4, NX, 16, CW), F32),
        pltpu.VMEM((4, NX, 16, CW), BF16),
        pltpu.VMEM((16, CW), BF16),
        pltpu.VMEM((2, MOVE, CW), BF16),
        pltpu.VMEM((2, MOVE, CW), BF16),
        pltpu.VMEM((2, CAP, CW), BF16),
        pltpu.VMEM((CAP, CW), BF16),
        pltpu.VMEM((NX, 1, 128), F32),
        pltpu.VMEM((4, 4, 1, 128), F32),
        pltpu.VMEM((2, 2, 16, CW), BF16),
        pltpu.VMEM((2, 2, 16, CW), BF16),
        pltpu.VMEM((2, 16, CW), F32),
        pltpu.VMEM((16, CW), F32),
        dma((6,)),
        dma((2,)),
        dma, dma,
        dma((3,)), dma((3,)), dma((4, 4)), dma((4, 4)), dma((3, 4)), dma((3, 4)),
        dma((3,)), dma((3,)), dma((4, 4)), dma((4, 4)), dma((3, 4)), dma((3, 4)),
        dma((2, 4)), dma((2, 4)), dma((2, 5)), dma((2, 5)),
        dma((3, 4)), dma((3, 4)), dma((3, 4)), dma((3, 4)), dma((4,)), dma((4,)),
        dma((3, 4)), dma((3, 4)), dma((3, 4)), dma((3, 4)), dma((4,)), dma((4,)),
        dma((3,)), dma((3,)), dma, dma,
        dma((12,)), dma((12,)),
    ]
    hidden, grad_up, grad_down = pl.pallas_call(
        kernel,
        out_shape=(
            jax.ShapeDtypeStruct((CAP, 2 * CW), BF16),
            jax.ShapeDtypeStruct((8, 2 * CW), F32),
            jax.ShapeDtypeStruct((8, 2 * CW), F32),
        ),
        in_specs=[hbm] * 6,
        out_specs=(hbm, vmem, vmem),
        scratch_shapes=scratch,
        compiler_params=pltpu.CompilerParams(
            collective_id=0, has_side_effects=True, vmem_limit_bytes=48 * 1024 * 1024
        ),
        cost_estimate=pl.CostEstimate(
            flops=4 * 10**9, bytes_accessed=2 * 1024 * 1024, transcendentals=262144
        ),
    )(
        *(
            pltpu.with_memory_space_constraint(a, pltpu.HBM)
            for a in (
                byte_states,
                cotangent,
                w_up,
                w_down.T,
                bounds.reshape(8, 128),
                owner_counts.reshape(1, 128),
            )
        )
    )
    return hidden, grad_up, grad_down.T


def solution(mesh):
    return jax.shard_map(
        body,
        mesh=mesh,
        in_specs=(
            P(("seq", "tp"), None),
            P(("seq", "tp"), None),
            P("seq", "tp"),
            P("tp", "seq"),
            P("seq"),
            P(),
        ),
        out_specs=(P("seq", "tp"), P("seq", "tp"), P("tp", "seq")),
        check_vma=False,
    )
```

```python
import functools

import jax
import jax.numpy as jnp
from jax import lax
from jax.experimental import pallas as pl
from jax.experimental.pallas import tpu as pltpu
from jax.sharding import PartitionSpec as P

MESH = pl.DeviceIdType.MESH
F32 = jnp.float32
BF16 = jnp.bfloat16

KLOC = 96
SLOT = 128
HALF = KLOC // 2
MOVE = 32
NX, NY, NZ = 4, 4, 16
BD = 256
DB = 1024
CW = 256
CAP = 512
NONE = -1.0e6
epsilon = 1e-05


def dot(a, b):
    return jnp.dot(a, b, preferred_element_type=F32)


def dot_nt(a, b):
    return lax.dot_general(a, b, (((1,), (1,)), ((), ())), preferred_element_type=F32)


def iota(shape, dim):
    return lax.broadcasted_iota(jnp.int32, shape, dim)


ORDER = (2, 1, 3, 0)


def kernel(
    bs_hbm, co_hbm, wu_hbm, wd_hbm, marks_hbm, oc_hbm,
    hid_hbm, g_out,
    bs, co, marks_in, oc_in, wu_in, wd_in, pw, rw, wur, wdr, wu, wd, xn, xc, nt, ct, hh, pg, ff,
    gu32, gub, gd32, gdb,
    ux, ua, ua2, ub, u1, u1b, u2b,
    dx, da, da2, db, d1, d1b, d2b,
    hs, hr, ho, hq, cx, cz, sb, rb, s0, r0,
    in_sem, out_sem,
    w_ss, w_rs,
    wuz_ss, wuz_rs, wua_ss, wua_rs, wux_ss, wux_rs,
    wdz_ss, wdz_rs, wda_ss, wda_rs, wdx_ss, wdx_rs,
    y_ss, y_rs, s_ss, s_rs,
    gux_ss, gux_rs, gua_ss, gua_rs, gub_ss, gub_rs,
    gdx_ss, gdx_rs, gda_ss, gda_rs, gdb_ss, gdb_rs,
    h_ss, h_rs, f_ss, f_rs, c_ss, c_rs,
):
    s = lax.axis_index("seq")
    t = lax.axis_index("tp")
    c = s % 2
    k = s // 2
    x = k % NX
    z = k // NX
    oc = 1 - c

    def at(zz, xx, cc, tt):
        return (((zz + NZ) % NZ * NX + (xx + NX) % NX) * 2 + cc, (tt + NY) % NY)

    sib = at(z, x, oc, t)
    yp, ym = at(z, x, c, t + 1), at(z, x, c, t - 1)
    xs = [at(z, x + 1, c, t), at(z, x - 1, c, t), at(z, x + 2, c, t)]
    z1p, z1m, z2p, z2m = (at(z + d, x, c, t) for d in (1, -1, 2, -2))
    z4p, z4m, z4p_other, z4m_other = (at(z + d, x, cc, t) for cc in (c, oc) for d in (4, -4))
    x_of = [(x + 1) % NX, (x + 3) % NX, (x + 2) % NX]
    nk = NZ * NX
    k_next = ((k + 1) % nk * 2 + c, t)
    k_prev = ((k + nk - 1) % nk * 2 + c, t)

    sends = []

    def send(src, dst, ss, rs, to):
        cp = pltpu.make_async_remote_copy(
            src_ref=src, dst_ref=dst, send_sem=ss, recv_sem=rs, device_id=to, device_id_type=MESH
        )
        cp.start()
        sends.append(cp)
        return cp

    peers = [sib, yp, ym] + xs + [z1p, z1m, z2p, z2m]
    peers += [z4p, z4m, z4p_other, z4m_other, k_next, k_prev]
    barrier = pltpu.get_barrier_semaphore()
    for p in peers:
        pl.semaphore_signal(barrier, inc=1, device_id=p, device_id_type=MESH)
    in_cps = [
        pltpu.make_async_copy(a, b, in_sem.at[i])
        for i, (a, b) in enumerate(
            (
                (marks_hbm, marks_in),
                (oc_hbm, oc_in),
                (bs_hbm, bs),
                (co_hbm, co),
                (wu_hbm, wu_in),
                (wd_hbm, wd_in),
            )
        )
    ]
    for cp in in_cps:
        cp.start()
    for i in (0, 4, 5):
        in_cps[i].wait()

    marks = marks_in[...].astype(F32)
    row8 = iota((8, 128), 0)
    lane8 = iota((8, 128), 1)
    per_row = jnp.sum(marks, axis=1, keepdims=True)
    own_counts = jnp.sum(
        jnp.where(row8 // 2 + 4 * c == lane8, per_row, 0.0), axis=0, keepdims=True
    )
    counts16 = jnp.broadcast_to(own_counts, (16, 128)).astype(BF16)
    both_w = jnp.concatenate([wu_in[...].astype(F32), wd_in[...].astype(F32)], axis=0).astype(BF16)
    for h in range(2):
        pw[h, :, 0:CW] = both_w[:, h * CW : (h + 1) * CW]
        pw[h, :, CW : CW + 128] = counts16

    pl.semaphore_wait(barrier, len(peers))
    w_cp = send(pw.at[oc], rw, w_ss, w_rs, sib)

    own_marks = jnp.concatenate(
        [
            jnp.sum(jnp.where(row8 == 2 * t + h, marks, 0.0), axis=0, keepdims=True)
            for h in range(2)
        ],
        axis=1,
    )
    upto = (iota((BD, BD), 0) <= iota((BD, BD), 1)).astype(F32).astype(BF16)
    rank = dot(jnp.broadcast_to(own_marks, (16, BD)).astype(BF16), upto)[0:1]
    slot_ids = iota((KLOC, BD), 0).astype(F32)
    in_span = jnp.where(slot_ids == rank - 1.0, 1.0, 0.0)
    segment = in_span.astype(BF16)
    select = (in_span * own_marks).astype(BF16)

    in_cps[2].wait()
    picked = dot(select, bs[...])
    inverse_rms = lax.rsqrt(jnp.mean(picked * picked, axis=1, keepdims=True) + epsilon)
    xn[c, t] = (picked * inverse_rms).astype(BF16)

    def send_own(buf, kind):
        own = buf.at[c, t]
        return (
            send(own, own, y_ss.at[kind, 0], y_rs.at[kind, 0], yp),
            send(own, own, y_ss.at[kind, 1], y_rs.at[kind, 1], ym),
            send(own, own, s_ss.at[kind, 0], s_rs.at[kind, 0], sib),
        )

    own_n = send_own(xn, 0)
    in_cps[3].wait()
    xc[c, t] = dot(segment, co[...]).astype(BF16)
    own_c = send_own(xc, 1)

    tp_, tm_, t2_ = (t + 1) % NY, (t + NY - 1) % NY, (t + 2) % NY

    def forward(buf, kind, own):
        own[0].wait_recv()
        a = buf.at[c, tm_, 0:HALF]
        f0 = send(a, a, y_ss.at[kind, 2], y_rs.at[kind, 2], yp)
        a = buf.at[c, tm_]
        g0 = send(a, a, s_ss.at[kind, 1], s_rs.at[kind, 1], sib)
        own[1].wait_recv()
        a = buf.at[c, tp_, HALF:KLOC]
        f1 = send(a, a, y_ss.at[kind, 3], y_rs.at[kind, 3], ym)
        a = buf.at[c, tp_]
        g1 = send(a, a, s_ss.at[kind, 2], s_rs.at[kind, 2], sib)
        return f0, f1, g0, g1

    def forward_far(buf, kind, f):
        f[0].wait_recv()
        a = buf.at[c, t2_, 0:HALF]
        g2 = send(a, a, s_ss.at[kind, 3], s_rs.at[kind, 3], sib)
        f[1].wait_recv()
        a = buf.at[c, t2_, HALF:KLOC]
        g3 = send(a, a, s_ss.at[kind, 4], s_rs.at[kind, 4], sib)
        return g2, g3

    eye = (iota((256, 256), 0) == iota((256, 256), 1)).astype(F32).astype(BF16)
    filler = jnp.zeros((SLOT - KLOC, DB), BF16)

    def rows_of(buf, cc, tt):
        return jnp.concatenate([buf[cc, tt], filler], axis=0)

    def transpose(buf, out, cc, tt):
        rows = rows_of(buf, cc, tt)
        for j in range(DB // 256):
            out[cc * 4 + tt, j * 256 : (j + 1) * 256, :] = dot_nt(
                eye, rows[:, j * 256 : (j + 1) * 256]
            ).astype(BF16)

    hh[:, KLOC:, :] = jnp.zeros((8, SLOT - KLOC, CW), BF16)
    pg[:, KLOC:, :] = jnp.zeros((8, SLOT - KLOC, CW), BF16)

    def up(cc):
        v = dot(xn[cc].reshape(NY * KLOC, DB), wu[...])
        sg = jax.nn.sigmoid(v)
        hh[pl.ds(cc * 4, 4), 0:KLOC, :] = (v * sg).astype(BF16).reshape(NY, KLOC, CW)
        ff[cc] = sg * (1.0 + v * (1.0 - sg))

    def back(cc):
        v = dot(xc[cc].reshape(NY * KLOC, DB), wd[...])
        pg[pl.ds(cc * 4, 4), 0:KLOC, :] = (v * ff[cc]).astype(BF16).reshape(NY, KLOC, CW)

    def arrive(cps):
        for cp in cps:
            cp.wait_recv()

    w_cp.wait_recv()
    mine, other = pw[c].astype(F32), rw[...].astype(F32)
    low, high = jnp.where(c == 0, mine, other), jnp.where(c == 0, other, mine)
    wur[0, 1, x] = jnp.concatenate([low[0:8, 0:CW], high[0:8, 0:CW]], axis=0).astype(BF16)
    wdr[0, 1, x] = jnp.concatenate([low[8:16, 0:CW], high[8:16, 0:CW]], axis=0).astype(BF16)
    cx[x] = low[0:1, CW:] + high[0:1, CW:]

    def stride(src, dst, j, to):
        return [
            send(b.at[src, 1, x], b.at[dst, 1, x], ss.at[j], rs.at[j], to)
            for b, ss, rs in ((wur, wuz_ss, wuz_rs), (wdr, wdz_ss, wdz_rs))
        ]

    w_z = {3: stride(0, 3, 0, z4p), 1: stride(0, 1, 1, z4m)}
    c_x = [send(cx.at[x], cx.at[x], c_ss.at[j], c_rs.at[j], xs[j]) for j in range(3)]

    def spread_near(part, m, ss, rs):
        cps = {
            (m, 0): send(part(m, 1), part(m, 0), ss.at[0, m], rs.at[0, m], z1p),
            (m, 2): send(part(m, 1), part(m, 2), ss.at[1, m], rs.at[1, m], z1m),
        }
        for to, mm, j in ((z2p, {0: 3, 3: 2}, 2), (z2m, {0: 0, 1: 1}, 3)):
            if m in mm:
                cps[mm[m], 3] = send(part(m, 1), part(mm[m], 3), ss.at[j, m], rs.at[j, m], to)
        return cps

    def spread_x(a, m, ss, rs):
        return [send(a, a, ss.at[j, m], rs.at[j, m], xs[j]) for j in range(3)]

    near_u, near_d, side_u, side_d = {}, {}, {}, {}

    def first_step(m):
        if m:
            arrive(w_z[m])
            if m == 3:
                w_z[2] = stride(3, 2, 2, z4p)
        near_u.update(spread_near(lambda mm, e: wur.at[mm, e, x], m, wua_ss, wua_rs))
        side_d[m] = spread_x(wdr.at[m, 1, x], m, wdx_ss, wdx_rs)

    def second_step(m):
        arrive([near_u[m, e] for e in (0, 2, 3)])
        side_u[m] = spread_x(wur.at[m, :, x], m, wux_ss, wux_rs)
        arrive(side_d[m])
        near_d.update(spread_near(lambda mm, e: wdr.at[mm, e], m, wda_ss, wda_rs))

    def settle(buf, out):
        for m in range(4):
            for e in range(4):
                at_z = (z + 4 * m + e - 1 + NZ) % NZ
                out[pl.ds(pl.multiple_of(at_z * 64, 64), 64), :] = buf[m, e].reshape(64, out.shape[1])

    first_step(0)
    arrive(c_x)
    lane1 = iota((1, 128), 1)
    here = cx[x]
    at_z_total = jnp.sum(cx[0] + cx[1] + cx[2] + cx[3], axis=1, keepdims=True)
    cz[0, 1] = jnp.broadcast_to(at_z_total, (1, 128))
    c_z = [
        send(cz.at[0, 1], cz.at[3, 1], c_ss.at[3], c_rs.at[3], z4p),
        send(cz.at[0, 1], cz.at[1, 1], c_ss.at[4], c_rs.at[4], z4m),
    ]
    transpose(xn, nt, c, t)
    transpose(xc, ct, c, t)
    first_step(3)
    first_step(1)
    arrive(c_z)
    c_far = send(cz.at[3, 1], cz.at[2, 1], c_ss.at[5], c_rs.at[5], z4p)
    second_step(0)
    far_n = forward(xn, 0, own_n)
    first_step(2)
    c_far.wait_recv()
    c_near = [
        send(cz.at[:, 1], cz.at[:, 0], c_ss.at[6], c_rs.at[6], z1p),
        send(cz.at[:, 1], cz.at[:, 2], c_ss.at[7], c_rs.at[7], z1m),
    ] + [
        send(cz.at[a, 1], cz.at[b, 3], c_ss.at[j], c_rs.at[j], to)
        for j, a, b, to in ((8, 0, 3, z2p), (9, 3, 2, z2p), (10, 0, 0, z2m), (11, 1, 1, z2m))
    ]
    second_step(3)
    far_c = forward(xc, 1, own_c)
    second_step(1)
    second_step(2)
    own_n[2].wait_recv()
    transpose(xn, nt, oc, t)
    transpose(xn, nt, c, tm_)
    transpose(xn, nt, c, tp_)

    own_c[2].wait_recv()
    transpose(xc, ct, oc, t)
    transpose(xc, ct, c, tm_)
    transpose(xc, ct, c, tp_)
    far_n[2].wait_recv()
    far_n[3].wait_recv()
    transpose(xn, nt, oc, tm_)
    transpose(xn, nt, oc, tp_)

    last_n = forward_far(xn, 0, far_n)
    transpose(xn, nt, c, t2_)
    last_c = forward_far(xc, 1, far_c)
    far_c[2].wait_recv()
    far_c[3].wait_recv()
    transpose(xc, ct, oc, tm_)
    transpose(xc, ct, oc, tp_)
    last_n[0].wait_recv()
    last_n[1].wait_recv()
    transpose(xn, nt, oc, t2_)
    for m in range(4):
        arrive(side_u[m])
    settle(wur, wu)
    up(c)
    up(oc)
    transpose(xc, ct, c, t2_)
    for m in range(4):
        arrive([near_d[m, e] for e in (0, 2, 3)])
    settle(wdr, wd)
    back(c)

    arrive(c_near)
    before = jnp.zeros((1, 128), F32)
    for m in range(4):
        for e in range(4):
            before = before + jnp.where((z + 4 * m + e - 1 + NZ) % NZ < z, cz[m, e], 0.0)
    beside = jnp.zeros((1, 128), F32)
    for xx in range(NX):
        beside = beside + jnp.where(xx < x, cx[xx], 0.0)
    before_a = before[:, 0:1] + jnp.sum(beside, axis=1, keepdims=True)
    slot1 = lane1.astype(F32)
    pos, totals = [], []
    for g in range(2):
        first = jnp.zeros((1, 1), F32)
        parts = []
        for p in range(4):
            n = jnp.sum(jnp.where(lane1 == 4 * g + p, here, 0.0), axis=1, keepdims=True)
            parts.append(jnp.where(slot1 < n, slot1 + first, NONE))
            first = first + n
        pos.append(jnp.concatenate(parts, axis=1))
        totals.append(first)
    in_cps[1].wait()
    owners = oc_in[...].astype(F32)
    owner_first = jnp.sum(jnp.where(lane1 < 2 * k, owners, 0.0), axis=1, keepdims=True)
    owned = [
        jnp.sum(jnp.where(lane1 == 2 * k + g, owners, 0.0), axis=1, keepdims=True)
        for g in range(2)
    ]
    shift = [owner_first - before_a, owner_first + owned[0] - before_a - totals[0]]
    end_ids = iota((MOVE, CAP), 0).astype(F32)
    group_rows = [hh[4 * g : 4 * g + 4].reshape(CAP, CW) for g in range(2)]

    def ends(g, base):
        table = jnp.where(end_ids + base == pos[g], 1.0, 0.0).astype(BF16)
        return dot(table, group_rows[g]).astype(BF16)

    hs[0] = ends(0, 0.0)
    hs[1] = ends(1, totals[1] - MOVE)
    h_p = send(hs.at[0], hr.at[0], h_ss.at[0], h_rs.at[0], k_prev)
    h_n = send(hs.at[1], hr.at[1], h_ss.at[1], h_rs.at[1], k_next)
    first_b = ends(1, 0.0)
    last_a = ends(0, totals[0] - MOVE)

    row_ids = iota((CAP, CAP), 0).astype(F32)
    end_row = iota((CAP, 2 * MOVE), 0).astype(F32)
    end_lane1 = iota((1, 2 * MOVE), 1)
    end_at = end_lane1.astype(F32)

    def place(g, edge):
        inner = jnp.where(
            (row_ids + shift[g] == pos[g]) & (row_ids < owned[g]), 1.0, 0.0
        ).astype(BF16)
        end_pos = jnp.where(end_lane1 < MOVE, end_at - MOVE, end_at - MOVE + totals[g])
        outer = jnp.where(
            (end_row + shift[g] == end_pos) & (end_row < owned[g]), 1.0, 0.0
        ).astype(BF16)
        ho[g] = (dot(inner, group_rows[g]) + dot(outer, edge)).astype(BF16)


    last_c[0].wait_recv()
    last_c[1].wait_recv()
    transpose(xc, ct, oc, t2_)
    back(oc)

    def grad(m, left_ref, right_ref, g32, gb):
        rows = []
        for e in range(4):
            at_z = (z + 4 * m + e - 1 + NZ) % NZ
            part = pl.ds(pl.multiple_of(at_z * 64, 64), 64)
            rows.append(jnp.concatenate([left_ref[b, part, :] for b in range(8)], axis=1))
        r = dot(jnp.concatenate(rows, axis=0), right_ref[...].reshape(8 * SLOT, CW))
        r = r.reshape(4, NX, 16, CW)
        g32[m] = r
        gb[m] = r.astype(BF16)

    def near_sum(part, m, into, into2, ss, rs):
        to2 = z2p if m < 2 else z2m
        return [
            send(part(m, 2), into.at[0, m], ss.at[0, m], rs.at[0, m], z1p),
            send(part(m, 0), into.at[1, m], ss.at[1, m], rs.at[1, m], z1m),
            send(part(m, 3), into2.at[m], ss.at[2, m], rs.at[2, m], to2),
        ]

    def near_total(own, m, cps, into, into2):
        far = {0: (0, 3), 1: (1,), 2: (), 3: (2,)}[m]
        arrive(cps[m][0:2] + [cps[i][2] for i in far])
        r = own + into[0, m].astype(F32) + into[1, m].astype(F32)
        for i in far:
            r = r + into2[i].astype(F32)
        return r

    def side_total(own, m, cps, into):
        arrive(cps[m])
        return own + into[0, m].astype(F32) + into[1, m].astype(F32) + into[2, m].astype(F32)

    g_dn, g_ux, g_dx, g_un, part_d, part_u = {}, {}, {}, {}, {}, {}

    def start(m):
        grad(m, ct, hh, gd32, gdb)
        g_dn[m] = near_sum(lambda mm, e: gdb.at[mm, e], m, da, da2, gda_ss, gda_rs)
        grad(m, nt, pg, gu32, gub)
        g_ux[m] = [
            send(gub.at[m, :, x_of[j]], ux.at[j, m], gux_ss.at[j, m], gux_rs.at[j, m], xs[j])
            for j in range(3)
        ]

    def d_first(m):
        r = near_total(gd32[m, 1], m, g_dn, da, da2)
        d1[m] = r
        d1b[m] = r.astype(BF16)
        g_dx[m] = [
            send(d1b.at[m, x_of[j]], dx.at[j, m], gdx_ss.at[j, m], gdx_rs.at[j, m], xs[j])
            for j in range(3)
        ]

    def u_first(m):
        r = side_total(gu32[m, :, x], m, g_ux, ux)
        u1[m] = r
        u1b[m] = r.astype(BF16)
        g_un[m] = near_sum(lambda mm, e: u1b.at[mm, e], m, ua, ua2, gua_ss, gua_rs)

    def halves(m):
        return [
            jnp.concatenate([part_u[m][8 * h : 8 * h + 8], part_d[m][8 * h : 8 * h + 8]], axis=0)
            for h in range(2)
        ]

    g_far, g_end = [], {}

    def both_second(m):
        part_d[m] = side_total(d1[m, x], m, g_dx, dx)
        part_u[m] = near_total(u1[m, 1], m, g_un, ua, ua2)
        if m == 2:
            u2b[...] = part_u[m].astype(BF16)
            d2b[...] = part_d[m].astype(BF16)
            g_far.append(send(u2b, ub, gub_ss.at[0], gub_rs.at[0], z4p))
            g_far.append(send(d2b, db, gdb_ss.at[0], gdb_rs.at[0], z4p))
            return
        if m == 1:
            arrive(g_far)
            part_u[m] = part_u[m] + ub[...].astype(F32)
            part_d[m] = part_d[m] + db[...].astype(F32)
        h = halves(m)
        if m == 0:
            s0[0], s0[1] = h
            g_end[m] = [send(s0.at[oc], r0, f_ss, f_rs, sib)]
            return
        slot = {1: 0, 3: 1}[m]
        sb[slot, 0] = h[0].astype(BF16)
        sb[slot, 1] = h[1].astype(BF16)
        same, other = {1: (z4p, z4p_other), 3: (z4m, z4m_other)}[m]
        g_end[m] = [
            send(sb.at[slot, c], rb.at[slot, c], gub_ss.at[m], gub_rs.at[m], same),
            send(sb.at[slot, oc], rb.at[slot, c], gdb_ss.at[m], gdb_rs.at[m], other),
        ]

    def both_first(m):
        d_first(m)
        u_first(m)

    start(2)
    start(1)
    both_first(2)
    start(3)
    start(0)
    both_first(1)
    both_second(2)

    h_p.wait_recv()
    h_n.wait_recv()
    place(0, jnp.concatenate([hr[1], first_b], axis=0))
    place(1, jnp.concatenate([last_a, hr[0]], axis=0))
    h_s = send(ho.at[oc], hq, h_ss.at[2], h_rs.at[2], sib)
    out_own = pltpu.make_async_copy(
        ho.at[c], hid_hbm.at[:, pl.ds(pl.multiple_of(c * CW, CW), CW)], out_sem.at[0]
    )
    out_own.start()

    both_first(3)
    both_second(1)
    both_first(0)
    both_second(3)
    both_second(0)

    h_s.wait_recv()
    out_sib = pltpu.make_async_copy(
        hq, hid_hbm.at[:, pl.ds(pl.multiple_of(oc * CW, CW), CW)], out_sem.at[1]
    )
    out_sib.start()

    arrive(g_end[1] + g_end[3] + g_end[0])
    mine = s0[c] + rb[0, c].astype(F32) + rb[1, c].astype(F32)
    other = r0[...] + rb[0, oc].astype(F32) + rb[1, oc].astype(F32)
    low, high = jnp.where(c == 0, mine, other), jnp.where(c == 0, other, mine)
    g_out[:, 0:CW] = low
    g_out[:, CW:] = high

    for cp in sends:
        cp.wait_send()
    out_own.wait()
    out_sib.wait()


def body(byte_states, cotangent, w_up, w_down, bounds, owner_counts):
    vmem = pl.BlockSpec(memory_space=pltpu.VMEM)
    hbm = pl.BlockSpec(memory_space=pltpu.HBM)
    dma = pltpu.SemaphoreType.DMA
    parts = (4, 4, NX, 16, CW)
    scratch = [
        pltpu.VMEM((BD, DB), BF16),
        pltpu.VMEM((BD, DB), BF16),
        pltpu.VMEM((8, 128), jnp.int32),
        pltpu.VMEM((1, 128), jnp.int32),
        pltpu.VMEM((8, 2 * CW), BF16),
        pltpu.VMEM((8, 2 * CW), BF16),
        pltpu.VMEM((2, 16, CW + 128), BF16),
        pltpu.VMEM((16, CW + 128), BF16),
        pltpu.VMEM(parts, BF16),
        pltpu.VMEM(parts, BF16),
        pltpu.VMEM((DB, CW), BF16),
        pltpu.VMEM((DB, CW), BF16),
        pltpu.VMEM((2, NY, KLOC, DB), BF16),
        pltpu.VMEM((2, NY, KLOC, DB), BF16),
        pltpu.VMEM((8, DB, SLOT), BF16),
        pltpu.VMEM((8, DB, SLOT), BF16),
        pltpu.VMEM((8, SLOT, CW), BF16),
        pltpu.VMEM((8, SLOT, CW), BF16),
        pltpu.VMEM((2, NY * KLOC, CW), F32),
        pltpu.VMEM(parts, F32),
        pltpu.VMEM(parts, BF16),
        pltpu.VMEM(parts, F32),
        pltpu.VMEM(parts, BF16),
        pltpu.VMEM((3, 4, 4, 16, CW), BF16),
        pltpu.VMEM((2, 4, 16, CW), BF16),
        pltpu.VMEM((4, 16, CW), BF16),
        pltpu.VMEM((16, CW), BF16),
        pltpu.VMEM((4, 4, 16, CW), F32),
        pltpu.VMEM((4, 4, 16, CW), BF16),
        pltpu.VMEM((16, CW), BF16),
        pltpu.VMEM((3, 4, 16, CW), BF16),
        pltpu.VMEM((2, 4, NX, 16, CW), BF16),
        pltpu.VMEM((4, NX, 16, CW), BF16),
        pltpu.VMEM((16, CW), BF16),
        pltpu.VMEM((4, NX, 16, CW), F32),
        pltpu.VMEM((4, NX, 16, CW), BF16),
        pltpu.VMEM((16, CW), BF16),
        pltpu.VMEM((2, MOVE, CW), BF16),
        pltpu.VMEM((2, MOVE, CW), BF16),
        pltpu.VMEM((2, CAP, CW), BF16),
        pltpu.VMEM((CAP, CW), BF16),
        pltpu.VMEM((NX, 1, 128), F32),
        pltpu.VMEM((4, 4, 1, 128), F32),
        pltpu.VMEM((2, 2, 16, CW), BF16),
        pltpu.VMEM((2, 2, 16, CW), BF16),
        pltpu.VMEM((2, 16, CW), F32),
        pltpu.VMEM((16, CW), F32),
        dma((6,)),
        dma((2,)),
        dma, dma,
        dma((3,)), dma((3,)), dma((4, 4)), dma((4, 4)), dma((3, 4)), dma((3, 4)),
        dma((3,)), dma((3,)), dma((4, 4)), dma((4, 4)), dma((3, 4)), dma((3, 4)),
        dma((2, 4)), dma((2, 4)), dma((2, 5)), dma((2, 5)),
        dma((3, 4)), dma((3, 4)), dma((3, 4)), dma((3, 4)), dma((4,)), dma((4,)),
        dma((3, 4)), dma((3, 4)), dma((3, 4)), dma((3, 4)), dma((4,)), dma((4,)),
        dma((3,)), dma((3,)), dma, dma,
        dma((12,)), dma((12,)),
    ]
    hidden, grads = pl.pallas_call(
        kernel,
        out_shape=(
            jax.ShapeDtypeStruct((CAP, 2 * CW), BF16),
            jax.ShapeDtypeStruct((16, 2 * CW), F32),
        ),
        in_specs=[hbm] * 6,
        out_specs=(hbm, vmem),
        scratch_shapes=scratch,
        compiler_params=pltpu.CompilerParams(
            collective_id=0, has_side_effects=True, vmem_limit_bytes=48 * 1024 * 1024
        ),
        cost_estimate=pl.CostEstimate(
            flops=4 * 10**9, bytes_accessed=2 * 1024 * 1024, transcendentals=262144
        ),
    )(
        *(
            pltpu.with_memory_space_constraint(a, pltpu.HBM)
            for a in (
                byte_states,
                cotangent,
                w_up,
                w_down.T,
                bounds.reshape(8, 128),
                owner_counts.reshape(1, 128),
            )
        )
    )
    return hidden, grads[0:8], grads[8:16].T


def solution(mesh):
    return jax.shard_map(
        body,
        mesh=mesh,
        in_specs=(
            P(("seq", "tp"), None),
            P(("seq", "tp"), None),
            P("seq", "tp"),
            P("tp", "seq"),
            P("seq"),
            P(),
        ),
        out_specs=(P("seq", "tp"), P("seq", "tp"), P("tp", "seq")),
        check_vma=False,
    )
```
